256 devices in a mesh: section: 4 (over y), row: 8 (over x, core), col: 8 (over z).
Axes of the slice: x: 4, y: 4, z: 8, core: 2. Of those that a mesh axis runs over, the one named last changes fastest.
Arguments:
- latent: bfloat16 [16, 32, 128, 256], P('section', 'row', 'col'), may hold values from -6 to 6
- w_first: bfloat16 [3, 3, 3, 256, 256], replicated, may hold values from -0.078125 to 0.078125
- w_second: bfloat16 [3, 3, 3, 256, 128], replicated, may hold values from -0.078125 to 0.078125
- w_third: bfloat16 [3, 3, 3, 128, 128], replicated, may hold values from -0.109375 to 0.109375
Outputs:
- decoded: bfloat16 [16, 64, 256, 128], P('section', 'row', 'col')
The draws below stay inside these ranges and needn't reach their ends.
All inputs are finite; a program needn't handle non-finite values.
Results may differ from the reference program's by a relative error of at most 0.0057.
Values may be sent and summed in bfloat16 or wider, within the bound.
A program may use at most 64 MiB of HBM per device.

```python
import jax
import jax.numpy as jnp
from jax import lax

LAT_CH = 256
MID_CH = 128
FRAMES = 16
H = 32
W = 128


def levels(key, extent, pieces, low, largest):
    def one(dim, parts):
        draws = jax.random.uniform(jax.random.fold_in(jax.random.fold_in(key, 6), dim), (parts,), jnp.float32, low / len(pieces), largest / len(pieces))
        return jnp.repeat(jnp.exp(draws), extent[dim] // parts).reshape((-1,) + (1,) * (len(extent) - dim - 1))

    gain = one(*pieces[0])
    for cut in pieces[1:]:
        gain = gain * one(*cut)
    return gain


def bell_draw(own_key, dims, scale, limit, cuts=(), kind=jnp.bfloat16):
    values = jax.random.normal(own_key, dims, jnp.float32) * scale
    if len(cuts) > 0:
        values = levels(own_key, dims, cuts, -0.22, 0.18) * values
    return jnp.clip(values, min=-limit, max=limit).astype(kind)


def setup_inputs(seed: int = 0) -> dict:
    keys = jax.random.split(jax.random.key(seed), 5)
    return {
        "latent": bell_draw(keys[0], (FRAMES, H, W, LAT_CH), 1.0, 6.0, ((0, 4), (1, 8), (2, 8))),
        "w_first": bell_draw(keys[1], (3, 3, 3, LAT_CH, LAT_CH), (27 * LAT_CH) ** -0.5, 0.078125),
        "w_second": bell_draw(keys[2], (3, 3, 3, LAT_CH, MID_CH), (27 * LAT_CH) ** -0.5, 0.078125),
        "w_third": bell_draw(keys[3], (3, 3, 3, MID_CH, MID_CH), (27 * MID_CH) ** -0.5, 0.109375),
    }


def causal_conv(field, kernel):
    padded = jnp.pad(field, ((2, 0), (1, 1), (1, 1), (0, 0)))
    result = lax.conv_general_dilated(padded[None], kernel, (1, 1, 1), "VALID", dimension_numbers=("NDHWC", "DHWIO", "NDHWC"), precision=lax.Precision.HIGHEST)
    return result[0]


def upsample(field):
    frames, height, breadth, width = field.shape
    grown = jnp.broadcast_to(field[:, :, None, :, None, :], (frames, height, 2, breadth, 2, width))
    return grown.reshape(frames, 2 * height, 2 * breadth, width)


def reference(latent, w_first, w_second, w_third):
    first = causal_conv(latent.astype(jnp.float32), w_first.astype(jnp.float32)).astype(jnp.bfloat16)
    grown = jnp.maximum(upsample(first), 0)
    second = jnp.maximum(causal_conv(grown.astype(jnp.float32), w_second.astype(jnp.float32)), 0.0).astype(jnp.bfloat16)
    decoded = causal_conv(second.astype(jnp.float32), w_third.astype(jnp.float32))
    return decoded.astype(jnp.bfloat16)
```

```python
import functools

import jax
import jax.numpy as jnp
import numpy as np
from jax import lax
from jax.experimental import pallas as pl
from jax.experimental.pallas import tpu as pltpu
from jax.sharding import PartitionSpec as P

MESH = pl.DeviceIdType.MESH
BF16 = jnp.bfloat16
F32 = jnp.float32

T, R, C = 4, 4, 16
LAT, MID = 256, 128
DIRS = [(dr, dc) for dr in (-1, 0, 1) for dc in (-1, 0, 1) if (dr, dc) != (0, 0)]
GROUPS = {"A": (3, 5), "B1": (2, 3), "B0": (1, 2), "C": (0, 1)}
ORDER = {"A": 0, "B1": 1, "B0": 2, "C": 3}
TAPS = [(dr, dc) for dr in range(3) for dc in range(3)]


def selections():
    sel = np.zeros((2, 400, 224), np.float32)

    def source(t2, row, col):
        if 2 <= col < 18:
            return row * C + col - 2
        side = 0 if col < 2 else 1
        slot, r = (0, row + 2) if row < 2 else (1, row - 2) if row < 6 else (2, row - 6)
        base = 128 if side == 1 else 176
        return base + slot * 16 + r * 4 + t2 * 2 + (col if side == 0 else col - 18)

    for t2 in range(2):
        for row in range(8):
            for j in range(C):
                sel[t2, row * C + j, source(t2, row, j)] = 1
                sel[t2, 128 + row * C + j, source(t2, row, j + 1)] = 1
        for tap, (dr, dc) in enumerate(TAPS):
            for j in range(2):
                for r in range(6):
                    sel[t2, 256 + tap * 16 + j * 8 + r, source(t2, r + dr, 16 + j + dc)] = 1
    pack = np.zeros((32, 128), np.float32)
    for side in range(2):
        for r in range(R):
            for t2 in range(2):
                for c in range(2):
                    pack[side * 16 + r * 4 + t2 * 2 + c, t2 * 64 + r * C + c + 14 * side] = 1
    return sel.astype(jnp.bfloat16), pack.astype(jnp.bfloat16)


def kernel(
    sizes, latent, w1_hbm, w2_hbm, w3_hbm, sel_ref, pack_ref, out_ref,
    rc, halo, pack, m0, m1, e9, f0, f1, e2, s0, s1, w1, w2, w2e, w3e,
    send, recv, ysend, yrecv, local,
):
    sections, rows, cols = sizes
    s, r, c = (lax.axis_index(a) for a in ("section", "row", "col"))

    def device(ds, dr, dc):
        return (
            lax.rem(s + ds + sections, sections),
            lax.rem(r + dr + rows, rows),
            lax.rem(c + dc + cols, cols),
        )

    def inside(i, size):
        return jnp.logical_and(i >= 0, i < size)

    def spatial(group, k):
        dr, dc = DIRS[k]
        g0, g1 = GROUPS[group]
        n = ORDER[group]
        if dc == 0:
            src = rc.at[2 * g0 : 2 * g1, pl.ds(4 if dr == 1 else 2, 2)]
            dst = rc.at[2 * g0 : 2 * g1, pl.ds(0 if dr == 1 else 6, 2)]
        else:
            side = 1 if dc == 1 else 0
            src = pack.at[side, g0:g1]
            dst = halo.at[1 - side, 1 - dr, g0:g1]
        return pltpu.make_async_remote_copy(
            src_ref=src, dst_ref=dst, send_sem=send.at[n, k], recv_sem=recv.at[n, k],
            device_id=device(0, dr, dc), device_id_type=MESH,
        )

    def sends(k):
        dr, dc = DIRS[k]
        return jnp.logical_and(inside(r + dr, rows), inside(c + dc, cols))

    def receives(k):
        dr, dc = DIRS[k]
        return jnp.logical_and(inside(r - dr, rows), inside(c - dc, cols))

    def spatial_start(group):
        for k in range(8):
            @pl.when(sends(k))
            def _():
                spatial(group, k).start()

    def spatial_wait_recv(group):
        for k in range(8):
            @pl.when(receives(k))
            def _():
                spatial(group, k).wait_recv()

    def spatial_wait_send(group):
        for k in range(8):
            @pl.when(sends(k))
            def _():
                spatial(group, k).wait_send()

    def onward(n):
        src, dst = ((8, 4), (6, 2), (4, 0))[n]
        return pltpu.make_async_remote_copy(
            src_ref=rc.at[pl.ds(src, 2), 2:6], dst_ref=rc.at[pl.ds(dst, 2), 2:6],
            send_sem=ysend.at[n], recv_sem=yrecv.at[n],
            device_id=device(1, 0, 0), device_id_type=MESH,
        )

    def make_pack(g):
        own = rc[2 * g : 2 * g + 2, 2:6].reshape(2 * R * C, LAT)
        both = jnp.dot(pack_ref[...], own, preferred_element_type=F32).astype(BF16)
        pack[0, g] = both[0:16]
        pack[1, g] = both[16:32]

    tile = pltpu.make_async_copy(latent, rc.at[6:10, 2:6], local.at[0])
    tile.start()
    second_copy = pltpu.make_async_copy(w2_hbm, w2, local.at[1])
    second_copy.start()
    first_copy = pltpu.make_async_copy(w1_hbm, w1, local.at[2])
    first_copy.start()
    third_copies = []
    for n, (e, p, fi, fo) in enumerate(
        [(0, 0, 0, 0), (1, 0, 1, 0), (0, 0, 1, 1), (2, 1, 0, 0), (1, 1, 0, 1), (2, 1, 1, 1)]
    ):
        copy = pltpu.make_async_copy(
            w3_hbm.at[:, :, e],
            w3e.at[:, p, :, fi * MID : (fi + 1) * MID, fo * MID : (fo + 1) * MID],
            local.at[3 + n],
        )
        copy.start()
        third_copies.append(copy)

    barrier = pltpu.get_barrier_semaphore()
    partners = [(0, dr, dc) for dr, dc in DIRS] + [(1, 0, 0), (-1, 0, 0)]
    for d in partners:
        pl.semaphore_signal(barrier, inc=1, device_id=device(*d), device_id_type=MESH)

    tile.wait()
    make_pack(4)
    make_pack(3)
    pl.semaphore_wait(barrier, len(partners))

    @pl.when(s < sections - 1)
    def _():
        onward(0).start()

    spatial_start("A")

    @pl.when(s < sections - 1)
    def _():
        onward(1).start()

    @pl.when(r == 0)
    def _():
        rc[:, 0:2] = jnp.zeros((10, 2, C, LAT), BF16)
        halo[:, 0] = jnp.zeros((2, 5, 16, LAT), BF16)

    @pl.when(r == rows - 1)
    def _():
        rc[:, 6:8] = jnp.zeros((10, 2, C, LAT), BF16)
        halo[:, 2] = jnp.zeros((2, 5, 16, LAT), BF16)

    @pl.when(c == 0)
    def _():
        halo[0] = jnp.zeros((3, 5, 16, LAT), BF16)

    @pl.when(c == cols - 1)
    def _():
        halo[1] = jnp.zeros((3, 5, 16, LAT), BF16)

    @pl.when(s == 0)
    def _():
        rc[2:6] = jnp.zeros((4, 8, C, LAT), BF16)
        halo[:, :, 1:3] = jnp.zeros((2, 3, 2, 16, LAT), BF16)

    @pl.when(s <= 1)
    def _():
        rc[0:2] = jnp.zeros((2, 8, C, LAT), BF16)
        halo[:, :, 0:1] = jnp.zeros((2, 3, 1, 16, LAT), BF16)

    w3e[:, 0, :, 0:MID, MID:] = jnp.zeros((3, 3, MID, MID), BF16)
    w3e[:, 1, :, MID:, 0:MID] = jnp.zeros((3, 3, MID, MID), BF16)

    second_copy.wait()
    pick = {(0, 0): (0, 1), (0, 1): (2,), (1, 0): (0,), (1, 1): (1, 2)}

    @pl.loop(0, 3)
    def _(a):
        for fr in range(2):
            for q in range(2):
                column = []
                for e in range(3):
                    x = [w2[a, b, e].astype(F32) for b in pick[fr, q]]
                    column.append(functools.reduce(jnp.add, x))
                for fc in range(2):
                    for p in range(2):
                        x = functools.reduce(jnp.add, [column[e] for e in pick[fc, p]])
                        lane = (fr * 2 + fc) * MID
                        row = (q * 2 + p) * LAT
                        w2e[a, row : row + LAT, lane : lane + MID] = x.astype(BF16)

    def prepare(t):
        g, t2 = t // 2, t % 2
        rhs = jnp.concatenate(
            [rc[t].reshape(8 * C, LAT), halo[1, :, g].reshape(48, LAT), halo[0, :, g].reshape(48, LAT)],
            axis=0,
        )
        moved = jnp.dot(sel_ref[t2], rhs, preferred_element_type=F32).astype(BF16)
        m0[t] = moved[0:128].reshape(8, C, LAT)
        m1[t] = moved[128:256].reshape(8, C, LAT)
        for tap in range(9):
            e9[t, :, tap * LAT : (tap + 1) * LAT] = moved[256 + tap * 16 : 272 + tap * 16]

    row16 = lax.broadcasted_iota(jnp.int32, (16, 1), 0)
    top, bottom = r == 0, r == rows - 1
    leftmost, rightmost = c == 0, c == cols - 1

    def shifted_up(x, last):
        return jnp.where(row16 == 15, last, pltpu.roll(x, 15, 0))

    def conv1(f):
        shifts = (m0, m1, rc)
        blocks = []
        for a in range(3):
            for tap, (dr, dc) in enumerate(TAPS):
                x = shifts[dc]
                blocks.append(
                    jnp.concatenate(
                        [x[f + a, dr : dr + 6].reshape(96, LAT), x[f + 1 + a, dr : dr + 6].reshape(96, LAT),
                         e9[f + a, :, tap * LAT : (tap + 1) * LAT], e9[f + 1 + a, :, tap * LAT : (tap + 1) * LAT]],
                        axis=0,
                    )
                )
        lhs = jnp.concatenate(blocks, axis=1)
        total = jnp.dot(lhs, w1[...].reshape(27 * LAT, LAT), preferred_element_type=F32)
        total = jnp.maximum(total, 0.0)
        for i in range(2):
            main = total[i * 96 : i * 96 + 96].reshape(6, 16, LAT)
            edge = total[192 + i * 16 : 208 + i * 16]
            row8 = row16 % 8
            bad = jnp.logical_or(
                jnp.logical_or(jnp.logical_and(row8 == 0, top), jnp.logical_and(row8 == 5, bottom)),
                jnp.logical_and(row16 >= 8, rightmost),
            )
            edge = jnp.where(jnp.logical_or(bad, row8 >= 6), 0.0, edge)
            for q in range(6):
                bad = jnp.logical_and(row16 == 0, leftmost)
                if q == 0:
                    bad = jnp.logical_or(bad, top)
                if q == 5:
                    bad = jnp.logical_or(bad, bottom)
                x = jnp.where(bad, 0.0, main[q])
                f0[f + i, q] = x.astype(BF16)
                f1[f + i, q] = shifted_up(x, edge[q : q + 1]).astype(BF16)
            nothing = jnp.zeros((8, LAT), F32)
            for p in range(2):
                x = edge[p * 8 : p * 8 + 8]
                for q, y in ((0, x), (1, pltpu.roll(x, 7, 0))):
                    lane = (q * 2 + p) * LAT
                    e2[f + i, :, lane : lane + LAT] = jnp.concatenate([y, nothing], axis=0).astype(BF16)

    def conv2(f):
        shifts = (f0, f1)
        blocks = []
        for a in range(3):
            for q in range(2):
                for p in range(2):
                    x = shifts[p]
                    lane = (q * 2 + p) * LAT
                    blocks.append(
                        jnp.concatenate(
                            [x[f + a, q : q + 5].reshape(80, LAT), x[f + 1 + a, q : q + 5].reshape(80, LAT),
                             e2[f + a, :, lane : lane + LAT], e2[f + 1 + a, :, lane : lane + LAT]],
                            axis=0,
                        )
                    )
        lhs = jnp.concatenate(blocks, axis=1)
        total = jnp.dot(lhs, w2e[...].reshape(12 * LAT, 4 * MID), preferred_element_type=F32)
        total = jnp.maximum(total, 0.0)
        for i in range(2):
            for lane in range(4):
                fr, fc = lane // 2, lane % 2
                cut = slice(lane * MID, (lane + 1) * MID)
                edge = total[160 + i * 16 : 176 + i * 16, cut]
                bad = jnp.logical_and(row16 == (0 if fr == 0 else 4), top if fr == 0 else bottom)
                if fc == 1:
                    bad = jnp.logical_or(bad, rightmost)
                edge = jnp.where(bad, 0.0, edge)
                for q in range(5):
                    x = total[i * 80 + q * 16 : i * 80 + q * 16 + 16, cut]
                    if fc == 0:
                        x = jnp.where(jnp.logical_and(row16 == 0, leftmost), 0.0, x)
                    if fr == 0 and q == 0:
                        x = jnp.where(top, 0.0, x)
                    if fr == 1 and q == 4:
                        x = jnp.where(bottom, 0.0, x)
                    s0[f + i, q, :, cut] = x.astype(BF16)
                    s1[f + i, q, :, cut] = shifted_up(x, edge[q : q + 1]).astype(BF16)

    def conv3(f):
        shifts = (s0, s1)
        blocks = []
        for a in range(3):
            for p in range(2):
                for b in range(3):
                    parts = []
                    for parity in range(2):
                        q, fr = divmod(b + parity, 2)
                        for i in range(2):
                            x = shifts[p][f + i + a, q : q + 4, :, fr * 256 : fr * 256 + 256]
                            parts.append(x.reshape(64, 256))
                    blocks.append(jnp.concatenate(parts, axis=0))
        lhs = jnp.concatenate(blocks, axis=1)
        total = jnp.dot(lhs, w3e[...].reshape(18 * 256, 256), preferred_element_type=F32).astype(BF16)
        for parity in range(2):
            for i in range(2):
                for q in range(4):
                    at = parity * 128 + i * 64 + q * 16
                    out_ref[f + i, 2 * q + parity] = total[at : at + 16]

    spatial_wait_recv("A")
    for t in (8, 9, 6, 7):
        prepare(t)

    @pl.when(s > 0)
    def _():
        onward(0).wait_recv()

        @pl.when(s < sections - 1)
        def _():
            onward(2).start()

        make_pack(2)
        spatial_start("B1")

    first_copy.wait()
    conv1(6)

    @pl.when(s > 0)
    def _():
        onward(1).wait_recv()
        make_pack(1)
        spatial_start("B0")
        spatial_wait_recv("B1")

    prepare(4)
    prepare(5)
    conv1(4)
    conv2(4)

    @pl.when(s > 1)
    def _():
        onward(2).wait_recv()
        make_pack(0)
        spatial_start("C")

    @pl.when(s > 0)
    def _():
        spatial_wait_recv("B0")

    prepare(2)
    prepare(3)
    conv1(2)
    conv2(2)
    for copy in third_copies:
        copy.wait()
    conv3(2)

    @pl.when(s > 1)
    def _():
        spatial_wait_recv("C")

    prepare(0)
    prepare(1)
    conv1(0)
    conv2(0)
    conv3(0)

    spatial_wait_send("A")

    @pl.when(s < sections - 1)
    def _():
        onward(0).wait_send()
        onward(1).wait_send()

    @pl.when(s > 0)
    def _():
        spatial_wait_send("B1")
        spatial_wait_send("B0")

        @pl.when(s < sections - 1)
        def _():
            onward(2).wait_send()

    @pl.when(s > 1)
    def _():
        spatial_wait_send("C")


def solution(mesh):
    sizes = tuple(mesh.shape[a] for a in ("section", "row", "col"))
    sel, pack = selections()

    def per_device(latent, w_first, w_second, w_third):
        hbm = pl.BlockSpec(memory_space=pltpu.HBM)
        vmem = pl.BlockSpec(memory_space=pltpu.VMEM)
        out = pl.pallas_call(
            functools.partial(kernel, sizes),
            out_shape=jax.ShapeDtypeStruct((T, 2 * R, C, 2 * MID), BF16),
            in_specs=[hbm] * 4 + [vmem] * 2,
            out_specs=vmem,
            scratch_shapes=[
                pltpu.VMEM((10, 8, C, LAT), BF16),
                pltpu.VMEM((2, 3, 5, 16, LAT), BF16),
                pltpu.VMEM((2, 5, 16, LAT), BF16),
                pltpu.VMEM((10, 8, C, LAT), BF16),
                pltpu.VMEM((10, 8, C, LAT), BF16),
                pltpu.VMEM((10, 16, 9 * LAT), BF16),
                pltpu.VMEM((8, 6, 16, LAT), BF16),
                pltpu.VMEM((8, 6, 16, LAT), BF16),
                pltpu.VMEM((8, 16, 4 * LAT), BF16),
                pltpu.VMEM((6, 5, 16, 4 * MID), BF16),
                pltpu.VMEM((6, 5, 16, 4 * MID), BF16),
                pltpu.VMEM((3, 3, 3, LAT, LAT), BF16),
                pltpu.VMEM((3, 3, 3, LAT, MID), BF16),
                pltpu.VMEM((3, 4 * LAT, 4 * MID), BF16),
                pltpu.VMEM((3, 2, 3, 2 * MID, 2 * MID), BF16),
                pltpu.SemaphoreType.DMA((4, 8)),
                pltpu.SemaphoreType.DMA((4, 8)),
                pltpu.SemaphoreType.DMA((3,)),
                pltpu.SemaphoreType.DMA((3,)),
                pltpu.SemaphoreType.DMA((9,)),
            ],
            compiler_params=pltpu.CompilerParams(
                collective_id=0, has_side_effects=True, vmem_limit_bytes=56 * 1024 * 1024
            ),
            cost_estimate=pl.CostEstimate(flops=7 * 10**9, bytes_accessed=8 * 10**6, transcendentals=0),
            name="decoder_block",
        )(latent, w_first, w_second, w_third, jnp.asarray(sel), jnp.asarray(pack))
        return out.reshape(T, 2 * R, 2 * C, MID)

    spec = P("section", "row", "col", None)
    return jax.shard_map(
        per_device, mesh=mesh, in_specs=(spec, P(), P(), P()), out_specs=spec, check_vma=False
    )
```

```python
import functools

import jax
import jax.numpy as jnp
import numpy as np
from jax import lax
from jax.experimental import pallas as pl
from jax.experimental.pallas import tpu as pltpu
from jax.sharding import PartitionSpec as P

MESH = pl.DeviceIdType.MESH
BF16 = jnp.bfloat16
F32 = jnp.float32

T, R, C = 4, 4, 16
LAT, MID = 256, 128
DIRS = [(dr, dc) for dr in (-1, 0, 1) for dc in (-1, 0, 1) if (dr, dc) != (0, 0)]
GROUPS = {"A": (3, 5), "B1": (2, 3), "B0": (1, 2), "C": (0, 1)}
ORDER = {"A": 0, "B1": 1, "B0": 2, "C": 3}
TAPS = [(dr, dc) for dr in range(3) for dc in range(3)]


def selections():
    sel = np.zeros((2, 400, 224), np.float32)

    def source(t2, row, col):
        if 2 <= col < 18:
            return row * C + col - 2
        side = 0 if col < 2 else 1
        slot, r = (0, row + 2) if row < 2 else (1, row - 2) if row < 6 else (2, row - 6)
        base = 128 if side == 1 else 176
        return base + slot * 16 + r * 4 + t2 * 2 + (col if side == 0 else col - 18)

    for t2 in range(2):
        for row in range(8):
            for j in range(C):
                sel[t2, row * C + j, source(t2, row, j)] = 1
                sel[t2, 128 + row * C + j, source(t2, row, j + 1)] = 1
        for tap, (dr, dc) in enumerate(TAPS):
            for j in range(2):
                for r in range(6):
                    sel[t2, 256 + tap * 16 + j * 8 + r, source(t2, r + dr, 16 + j + dc)] = 1
    pack = np.zeros((32, 128), np.float32)
    for side in range(2):
        for r in range(R):
            for t2 in range(2):
                for c in range(2):
                    pack[side * 16 + r * 4 + t2 * 2 + c, t2 * 64 + r * C + c + 14 * side] = 1
    return sel.astype(jnp.bfloat16), pack.astype(jnp.bfloat16)


def kernel(
    sizes, latent, w1_hbm, w2_hbm, w3_hbm, sel_hbm, pack_ref, out_hbm,
    rc, halo, pack, m0, m1, e9, f0, f1, e2, s0, s1, w1, w2, w2e, w3e, sel_ref, out_ref, woven,
    send, recv, ysend, yrecv, local,
):
    sections, rows, cols = sizes
    s, r, c = (lax.axis_index(a) for a in ("section", "row", "col"))

    def device(ds, dr, dc):
        return (
            lax.rem(s + ds + sections, sections),
            lax.rem(r + dr + rows, rows),
            lax.rem(c + dc + cols, cols),
        )

    def inside(i, size):
        return jnp.logical_and(i >= 0, i < size)

    def spatial(group, k):
        dr, dc = DIRS[k]
        g0, g1 = GROUPS[group]
        n = ORDER[group]
        if dc == 0:
            src = rc.at[2 * g0 : 2 * g1, pl.ds(4 if dr == 1 else 2, 2)]
            dst = rc.at[2 * g0 : 2 * g1, pl.ds(0 if dr == 1 else 6, 2)]
        else:
            side = 1 if dc == 1 else 0
            src = pack.at[side, g0:g1]
            dst = halo.at[1 - side, 1 - dr, g0:g1]
        return pltpu.make_async_remote_copy(
            src_ref=src, dst_ref=dst, send_sem=send.at[n, k], recv_sem=recv.at[n, k],
            device_id=device(0, dr, dc), device_id_type=MESH,
        )

    def sends(k):
        dr, dc = DIRS[k]
        return jnp.logical_and(inside(r + dr, rows), inside(c + dc, cols))

    def receives(k):
        dr, dc = DIRS[k]
        return jnp.logical_and(inside(r - dr, rows), inside(c - dc, cols))

    def spatial_start(group):
        for k in range(8):
            @pl.when(sends(k))
            def _():
                spatial(group, k).start()

    def spatial_wait_recv(group):
        for k in range(8):
            @pl.when(receives(k))
            def _():
                spatial(group, k).wait_recv()

    def spatial_wait_send(group):
        for k in range(8):
            @pl.when(sends(k))
            def _():
                spatial(group, k).wait_send()

    def onward(n):
        src, dst = ((8, 4), (6, 2), (4, 0))[n]
        return pltpu.make_async_remote_copy(
            src_ref=rc.at[pl.ds(src, 2), 2:6], dst_ref=rc.at[pl.ds(dst, 2), 2:6],
            send_sem=ysend.at[n], recv_sem=yrecv.at[n],
            device_id=device(1, 0, 0), device_id_type=MESH,
        )

    def make_pack(g):
        own = rc[2 * g : 2 * g + 2, 2:6].reshape(2 * R * C, LAT)
        both = jnp.dot(pack_ref[...], own, preferred_element_type=F32).astype(BF16)
        pack[0, g] = both[0:16]
        pack[1, g] = both[16:32]

    tile = pltpu.make_async_copy(latent, rc.at[6:10, 2:6], local.at[0])
    tile.start()
    sel_copy = pltpu.make_async_copy(sel_hbm, sel_ref, local.at[11])
    sel_copy.start()
    second_copy = pltpu.make_async_copy(w2_hbm, w2, local.at[1])
    second_copy.start()
    first_copy = pltpu.make_async_copy(w1_hbm, w1, local.at[2])
    first_copy.start()
    third_copies = []
    for n, (e, p, fi, fo) in enumerate(
        [(0, 0, 0, 0), (1, 0, 1, 0), (0, 0, 1, 1), (2, 1, 0, 0), (1, 1, 0, 1), (2, 1, 1, 1)]
    ):
        copy = pltpu.make_async_copy(
            w3_hbm.at[:, :, e],
            w3e.at[:, p, :, fi * MID : (fi + 1) * MID, fo * MID : (fo + 1) * MID],
            local.at[3 + n],
        )
        copy.start()
        third_copies.append(copy)

    barrier = pltpu.get_barrier_semaphore()
    partners = [(0, dr, dc) for dr, dc in DIRS] + [(1, 0, 0), (-1, 0, 0)]
    for d in partners:
        pl.semaphore_signal(barrier, inc=1, device_id=device(*d), device_id_type=MESH)

    tile.wait()
    make_pack(4)
    make_pack(3)
    pl.semaphore_wait(barrier, len(partners))

    @pl.when(s < sections - 1)
    def _():
        onward(0).start()

    spatial_start("A")

    @pl.when(s < sections - 1)
    def _():
        onward(1).start()

    @pl.when(r == 0)
    def _():
        rc[:, 0:2] = jnp.zeros((10, 2, C, LAT), BF16)
        halo[:, 0] = jnp.zeros((2, 5, 16, LAT), BF16)

    @pl.when(r == rows - 1)
    def _():
        rc[:, 6:8] = jnp.zeros((10, 2, C, LAT), BF16)
        halo[:, 2] = jnp.zeros((2, 5, 16, LAT), BF16)

    @pl.when(c == 0)
    def _():
        halo[0] = jnp.zeros((3, 5, 16, LAT), BF16)

    @pl.when(c == cols - 1)
    def _():
        halo[1] = jnp.zeros((3, 5, 16, LAT), BF16)

    @pl.when(s == 0)
    def _():
        rc[2:6] = jnp.zeros((4, 8, C, LAT), BF16)
        halo[:, :, 1:3] = jnp.zeros((2, 3, 2, 16, LAT), BF16)

    @pl.when(s <= 1)
    def _():
        rc[0:2] = jnp.zeros((2, 8, C, LAT), BF16)
        halo[:, :, 0:1] = jnp.zeros((2, 3, 1, 16, LAT), BF16)

    w3e[:, 0, :, 0:MID, MID:] = jnp.zeros((3, 3, MID, MID), BF16)
    w3e[:, 1, :, MID:, 0:MID] = jnp.zeros((3, 3, MID, MID), BF16)

    second_copy.wait()
    pick = {(0, 0): (0, 1), (0, 1): (2,), (1, 0): (0,), (1, 1): (1, 2)}

    @pl.loop(0, 3)
    def _(a):
        for fr in range(2):
            for q in range(2):
                column = []
                for e in range(3):
                    x = [w2[a, b, e].astype(F32) for b in pick[fr, q]]
                    column.append(functools.reduce(jnp.add, x))
                for fc in range(2):
                    for p in range(2):
                        x = functools.reduce(jnp.add, [column[e] for e in pick[fc, p]])
                        lane = (fr * 2 + fc) * MID
                        row = (q * 2 + p) * LAT
                        w2e[a, row : row + LAT, lane : lane + MID] = x.astype(BF16)

    def prepare(t):
        g, t2 = t // 2, lax.rem(t, 2)
        rhs = jnp.concatenate(
            [rc[t].reshape(8 * C, LAT), halo[1, :, g].reshape(48, LAT), halo[0, :, g].reshape(48, LAT)],
            axis=0,
        )
        moved = jnp.dot(sel_ref[t2], rhs, preferred_element_type=F32).astype(BF16)
        m0[t] = moved[0:128].reshape(8, C, LAT)
        m1[t] = moved[128:256].reshape(8, C, LAT)
        for tap in range(9):
            e9[t, :, tap * LAT : (tap + 1) * LAT] = moved[256 + tap * 16 : 272 + tap * 16]

    row16 = lax.broadcasted_iota(jnp.int32, (16, 1), 0)
    top, bottom = r == 0, r == rows - 1
    leftmost, rightmost = c == 0, c == cols - 1

    def shifted_up(x, last):
        return jnp.where(row16 == 15, last, pltpu.roll(x, 15, 0))

    def result(f):
        return pltpu.make_async_copy(
            out_ref.at[pl.ds(f, 2)], out_hbm.at[pl.ds(f, 2)], local.at[9 + f // 2]
        )

    def conv1(f):
        shifts = (m0, m1, rc)
        blocks = []
        for a in range(3):
            for tap, (dr, dc) in enumerate(TAPS):
                x = shifts[dc]
                blocks.append(
                    jnp.concatenate(
                        [x[f + a, dr : dr + 6].reshape(96, LAT), x[f + 1 + a, dr : dr + 6].reshape(96, LAT),
                         e9[f + a, :, tap * LAT : (tap + 1) * LAT], e9[f + 1 + a, :, tap * LAT : (tap + 1) * LAT]],
                        axis=0,
                    )
                )
        lhs = jnp.concatenate(blocks, axis=1)
        total = jnp.dot(lhs, w1[...].reshape(27 * LAT, LAT), preferred_element_type=F32)
        total = jnp.maximum(total, 0.0)
        for i in range(2):
            main = total[i * 96 : i * 96 + 96].reshape(6, 16, LAT)
            edge = total[192 + i * 16 : 208 + i * 16]
            row8 = row16 % 8
            bad = jnp.logical_or(
                jnp.logical_or(jnp.logical_and(row8 == 0, top), jnp.logical_and(row8 == 5, bottom)),
                jnp.logical_and(row16 >= 8, rightmost),
            )
            edge = jnp.where(jnp.logical_or(bad, row8 >= 6), 0.0, edge)
            for q in range(6):
                bad = jnp.logical_and(row16 == 0, leftmost)
                if q == 0:
                    bad = jnp.logical_or(bad, top)
                if q == 5:
                    bad = jnp.logical_or(bad, bottom)
                x = jnp.where(bad, 0.0, main[q])
                f0[f + i, q] = x.astype(BF16)
                f1[f + i, q] = shifted_up(x, edge[q : q + 1]).astype(BF16)
            nothing = jnp.zeros((8, LAT), F32)
            for p in range(2):
                x = edge[p * 8 : p * 8 + 8]
                for q, y in ((0, x), (1, pltpu.roll(x, 7, 0))):
                    lane = (q * 2 + p) * LAT
                    e2[f + i, :, lane : lane + LAT] = jnp.concatenate([y, nothing], axis=0).astype(BF16)

    def conv2(f):
        shifts = (f0, f1)
        blocks = []
        for a in range(3):
            for q in range(2):
                for p in range(2):
                    x = shifts[p]
                    lane = (q * 2 + p) * LAT
                    blocks.append(
                        jnp.concatenate(
                            [x[f + a, q : q + 5].reshape(80, LAT), x[f + 1 + a, q : q + 5].reshape(80, LAT),
                             e2[f + a, :, lane : lane + LAT], e2[f + 1 + a, :, lane : lane + LAT]],
                            axis=0,
                        )
                    )
        lhs = jnp.concatenate(blocks, axis=1)
        total = jnp.dot(lhs, w2e[...].reshape(12 * LAT, 4 * MID), preferred_element_type=F32)
        total = jnp.maximum(total, 0.0)
        for i in range(2):
            for lane in range(4):
                fr, fc = lane // 2, lane % 2
                cut = slice(lane * MID, (lane + 1) * MID)
                edge = total[160 + i * 16 : 176 + i * 16, cut]
                bad = jnp.logical_and(row16 == (0 if fr == 0 else 4), top if fr == 0 else bottom)
                if fc == 1:
                    bad = jnp.logical_or(bad, rightmost)
                edge = jnp.where(bad, 0.0, edge)
                for q in range(5):
                    x = total[i * 80 + q * 16 : i * 80 + q * 16 + 16, cut]
                    if fc == 0:
                        x = jnp.where(jnp.logical_and(row16 == 0, leftmost), 0.0, x)
                    if fr == 0 and q == 0:
                        x = jnp.where(top, 0.0, x)
                    if fr == 1 and q == 4:
                        x = jnp.where(bottom, 0.0, x)
                    s0[f + i, q, :, cut] = x.astype(BF16)
                    s1[f + i, q, :, cut] = shifted_up(x, edge[q : q + 1]).astype(BF16)

    def conv3(f):
        shifts = (s0, s1)
        blocks = []
        for a in range(3):
            for p in range(2):
                for b in range(3):
                    parts = []
                    for parity in range(2):
                        q, fr = divmod(b + parity, 2)
                        for i in range(2):
                            x = shifts[p][f + i + a, q : q + 4, :, fr * 256 : fr * 256 + 256]
                            parts.append(x.reshape(64, 256))
                    blocks.append(jnp.concatenate(parts, axis=0))
        lhs = jnp.concatenate(blocks, axis=1)
        total = jnp.dot(lhs, w3e[...].reshape(18 * 256, 256), preferred_element_type=F32)
        for parity in range(2):
            for i in range(2):
                for q in range(4):
                    at = parity * 128 + i * 64 + q * 16
                    for fc in range(2):
                        woven[fc::2] = total[at : at + 16, fc * MID : (fc + 1) * MID]
                    out_ref[f + i, 2 * q + parity] = woven[...].astype(BF16)

    sel_copy.wait()
    spatial_wait_recv("A")

    @pl.loop(8, 10)
    def _(t):
        prepare(t)

    @pl.loop(0, 4)
    def _(i):
        f = 6 - 2 * i

        @pl.when(jnp.logical_and(i == 0, s > 0))
        def _():
            onward(0).wait_recv()

            @pl.when(s < sections - 1)
            def _():
                onward(2).start()

            make_pack(2)
            spatial_start("B1")

        @pl.when(jnp.logical_and(i == 1, s > 0))
        def _():
            onward(1).wait_recv()
            make_pack(1)
            spatial_start("B0")
            spatial_wait_recv("B1")

        @pl.when(jnp.logical_and(i == 2, s > 1))
        def _():
            onward(2).wait_recv()
            make_pack(0)
            spatial_start("C")

        @pl.when(jnp.logical_and(i == 2, s > 0))
        def _():
            spatial_wait_recv("B0")

        @pl.when(jnp.logical_and(i == 3, s > 1))
        def _():
            spatial_wait_recv("C")

        @pl.loop(0, 2)
        def _(k):
            prepare(f + k)

        @pl.when(i == 0)
        def _():
            first_copy.wait()

        conv1(f)

        @pl.when(i >= 1)
        def _():
            conv2(f)

        @pl.when(i == 2)
        def _():
            for copy in third_copies:
                copy.wait()

        @pl.when(i >= 2)
        def _():
            conv3(f)
            result(f).start()

    result(2).wait()
    result(0).wait()

    spatial_wait_send("A")

    @pl.when(s < sections - 1)
    def _():
        onward(0).wait_send()
        onward(1).wait_send()

    @pl.when(s > 0)
    def _():
        spatial_wait_send("B1")
        spatial_wait_send("B0")

        @pl.when(s < sections - 1)
        def _():
            onward(2).wait_send()

    @pl.when(s > 1)
    def _():
        spatial_wait_send("C")


def solution(mesh):
    sizes = tuple(mesh.shape[a] for a in ("section", "row", "col"))
    sel, pack = selections()

    def per_device(latent, w_first, w_second, w_third):
        hbm = pl.BlockSpec(memory_space=pltpu.HBM)
        vmem = pl.BlockSpec(memory_space=pltpu.VMEM)
        out = pl.pallas_call(
            functools.partial(kernel, sizes),
            out_shape=jax.ShapeDtypeStruct((T, 2 * R, 2 * C, MID), BF16),
            in_specs=[hbm] * 5 + [vmem],
            out_specs=hbm,
            scratch_shapes=[
                pltpu.VMEM((10, 8, C, LAT), BF16),
                pltpu.VMEM((2, 3, 5, 16, LAT), BF16),
                pltpu.VMEM((2, 5, 16, LAT), BF16),
                pltpu.VMEM((10, 8, C, LAT), BF16),
                pltpu.VMEM((10, 8, C, LAT), BF16),
                pltpu.VMEM((10, 16, 9 * LAT), BF16),
                pltpu.VMEM((8, 6, 16, LAT), BF16),
                pltpu.VMEM((8, 6, 16, LAT), BF16),
                pltpu.VMEM((8, 16, 4 * LAT), BF16),
                pltpu.VMEM((6, 5, 16, 4 * MID), BF16),
                pltpu.VMEM((6, 5, 16, 4 * MID), BF16),
                pltpu.VMEM((3, 3, 3, LAT, LAT), BF16),
                pltpu.VMEM((3, 3, 3, LAT, MID), BF16),
                pltpu.VMEM((3, 4 * LAT, 4 * MID), BF16),
                pltpu.VMEM((3, 2, 3, 2 * MID, 2 * MID), BF16),
                pltpu.VMEM((2, 400, 224), BF16),
                pltpu.VMEM((T, 2 * R, 2 * C, MID), BF16),
                pltpu.VMEM((2 * C, MID), F32),
                pltpu.SemaphoreType.DMA((4, 8)),
                pltpu.SemaphoreType.DMA((4, 8)),
                pltpu.SemaphoreType.DMA((3,)),
                pltpu.SemaphoreType.DMA((3,)),
                pltpu.SemaphoreType.DMA((12,)),
            ],
            compiler_params=pltpu.CompilerParams(
                collective_id=0, has_side_effects=True, vmem_limit_bytes=56 * 1024 * 1024
            ),
            cost_estimate=pl.CostEstimate(flops=7 * 10**9, bytes_accessed=8 * 10**6, transcendentals=0),
            name="decoder_block",
        )(latent, w_first, w_second, w_third, jnp.asarray(sel), jnp.asarray(pack))
        return out

    spec = P("section", "row", "col", None)
    return jax.shard_map(
        per_device, mesh=mesh, in_specs=(spec, P(), P(), P()), out_specs=spec, check_vma=False
    )
```

```python
import functools

import jax
import jax.numpy as jnp
import numpy as np
from jax import lax
from jax.experimental import pallas as pl
from jax.experimental.pallas import tpu as pltpu
from jax.sharding import PartitionSpec as P

MESH = pl.DeviceIdType.MESH
BF16 = jnp.bfloat16
F32 = jnp.float32

T, R, C = 4, 4, 16
LAT, MID = 256, 128
DIRS = [(-1, 0), (1, 0), (-1, -1), (-1, 1), (1, -1), (1, 1), (0, -1), (0, 1)]
GROUPS = {"A": (3, 5), "B1": (2, 3), "B0": (1, 2), "C": (0, 1)}
ORDER = {"A": 0, "B1": 1, "B0": 2, "C": 3}
TAPS = [(dr, dc) for dr in range(3) for dc in range(3)]


def selections():
    sel = np.zeros((2, 144, 176), np.float32)

    def source(t2, row, col):
        if col < 18:
            return row * C + col - 2
        slot, r = (0, row + 2) if row < 2 else (1, row - 2) if row < 6 else (2, row - 6)
        return 128 + slot * 16 + r * 4 + t2 * 2 + col - 18

    for t2 in range(2):
        for tap, (dr, dc) in enumerate(TAPS):
            for j in range(2):
                for r in range(6):
                    sel[t2, tap * 16 + j * 8 + r, source(t2, r + dr, 16 + j + dc)] = 1
    pack = np.zeros((32, 128), np.float32)
    for side in range(2):
        for r in range(R):
            for t2 in range(2):
                for c in range(2):
                    pack[side * 16 + r * 4 + t2 * 2 + c, t2 * 64 + r * C + c + 14 * side] = 1
    return sel.astype(jnp.bfloat16), pack.astype(jnp.bfloat16)


def kernel(
    sizes, latent, w1_hbm, w2_hbm, w3_hbm, sel_hbm, pick_hbm, out_ref,
    rc, halo, pack, m0, m1, e9, f0, f1, e2, s0, s1, w1, w2, w2e, w3e, sel_ref, pick_ref, woven,
    send, recv, ysend, yrecv, local,
):
    sections, rows, cols = sizes
    s, r, c = (lax.axis_index(a) for a in ("section", "row", "col"))

    def device(ds, dr, dc):
        return (
            lax.rem(s + ds + sections, sections),
            lax.rem(r + dr + rows, rows),
            lax.rem(c + dc + cols, cols),
        )

    def inside(i, size):
        return jnp.logical_and(i >= 0, i < size)

    def spatial(group, k):
        dr, dc = DIRS[k]
        g0, g1 = GROUPS[group]
        n = ORDER[group]
        if dc == 0:
            src = rc.at[2 * g0 : 2 * g1, pl.ds(4 if dr == 1 else 2, 2)]
            dst = rc.at[2 * g0 : 2 * g1, pl.ds(0 if dr == 1 else 6, 2)]
        else:
            side = 1 if dc == 1 else 0
            src = pack.at[side, g0:g1]
            dst = halo.at[1 - side, 1 - dr, g0:g1]
        return pltpu.make_async_remote_copy(
            src_ref=src, dst_ref=dst, send_sem=send.at[n, k], recv_sem=recv.at[n, k],
            device_id=device(0, dr, dc), device_id_type=MESH,
        )

    def sends(k):
        dr, dc = DIRS[k]
        return jnp.logical_and(inside(r + dr, rows), inside(c + dc, cols))

    def receives(k):
        dr, dc = DIRS[k]
        return jnp.logical_and(inside(r - dr, rows), inside(c - dc, cols))

    def spatial_start(group):
        for k in range(8):
            if k == 2 and group != "A":
                make_pack(GROUPS[group][0])

            @pl.when(sends(k))
            def _():
                spatial(group, k).start()

    def spatial_wait_recv(group):
        for k in range(8):
            @pl.when(receives(k))
            def _():
                spatial(group, k).wait_recv()

    def spatial_wait_send(group):
        for k in range(8):
            @pl.when(sends(k))
            def _():
                spatial(group, k).wait_send()

    def onward(n):
        src, dst = ((8, 4), (6, 2), (4, 0))[n]
        return pltpu.make_async_remote_copy(
            src_ref=rc.at[pl.ds(src, 2), 2:6], dst_ref=rc.at[pl.ds(dst, 2), 2:6],
            send_sem=ysend.at[n], recv_sem=yrecv.at[n],
            device_id=device(1, 0, 0), device_id_type=MESH,
        )

    def make_pack(g):
        own = rc[2 * g : 2 * g + 2, 2:6].reshape(2 * R * C, LAT)
        both = jnp.dot(pick_ref[...], own, preferred_element_type=F32).astype(BF16)
        pack[0, g] = both[0:16]
        pack[1, g] = both[16:32]

    barrier = pltpu.get_barrier_semaphore()
    partners = [(-1, 0, 0)] + [(0, dr, dc) for dr, dc in reversed(DIRS)] + [(1, 0, 0)]
    for d in partners:
        pl.semaphore_signal(barrier, inc=1, device_id=device(*d), device_id_type=MESH)

    tile = pltpu.make_async_copy(latent, rc.at[6:10, 2:6], local.at[0])
    tile.start()
    sel_copy = pltpu.make_async_copy(sel_hbm, sel_ref, local.at[10])
    sel_copy.start()
    pick_copy = pltpu.make_async_copy(pick_hbm, pick_ref, local.at[9])
    pick_copy.start()
    second_copy = pltpu.make_async_copy(w2_hbm, w2, local.at[1])
    second_copy.start()
    first_copy = pltpu.make_async_copy(w1_hbm, w1, local.at[2])
    first_copy.start()
    third_copies = []
    for n, (e, p, fi, fo) in enumerate(
        [(0, 0, 0, 0), (1, 0, 1, 0), (0, 0, 1, 1), (2, 1, 0, 0), (1, 1, 0, 1), (2, 1, 1, 1)]
    ):
        copy = pltpu.make_async_copy(
            w3_hbm.at[:, :, e],
            w3e.at[:, p, :, fi * MID : (fi + 1) * MID, fo * MID : (fo + 1) * MID],
            local.at[3 + n],
        )
        copy.start()
        third_copies.append(copy)

    tile.wait()
    pick_copy.wait()
    make_pack(4)
    make_pack(3)
    pl.semaphore_wait(barrier, len(partners))

    @pl.when(s < sections - 1)
    def _():
        onward(0).start()

    spatial_start("A")

    @pl.when(s < sections - 1)
    def _():
        onward(1).start()

    @pl.when(r == 0)
    def _():
        rc[:, 0:2] = jnp.zeros((10, 2, C, LAT), BF16)
        halo[:, 0] = jnp.zeros((2, 5, 16, LAT), BF16)

    @pl.when(r == rows - 1)
    def _():
        rc[:, 6:8] = jnp.zeros((10, 2, C, LAT), BF16)
        halo[:, 2] = jnp.zeros((2, 5, 16, LAT), BF16)

    @pl.when(c == 0)
    def _():
        halo[0] = jnp.zeros((3, 5, 16, LAT), BF16)

    @pl.when(c == cols - 1)
    def _():
        halo[1] = jnp.zeros((3, 5, 16, LAT), BF16)

    @pl.when(s == 0)
    def _():
        rc[2:6] = jnp.zeros((4, 8, C, LAT), BF16)
        halo[:, :, 1:3] = jnp.zeros((2, 3, 2, 16, LAT), BF16)

    @pl.when(s <= 1)
    def _():
        rc[0:2] = jnp.zeros((2, 8, C, LAT), BF16)
        halo[:, :, 0:1] = jnp.zeros((2, 3, 1, 16, LAT), BF16)

    w3e[:, 0, :, 0:MID, MID:] = jnp.zeros((3, 3, MID, MID), BF16)
    w3e[:, 1, :, MID:, 0:MID] = jnp.zeros((3, 3, MID, MID), BF16)

    second_copy.wait()
    pick = {(0, 0): (0, 1), (0, 1): (2,), (1, 0): (0,), (1, 1): (1, 2)}

    @pl.loop(0, 3)
    def _(a):
        for fr in range(2):
            for q in range(2):
                column = []
                for e in range(3):
                    x = [w2[a, b, e].astype(F32) for b in pick[fr, q]]
                    column.append(functools.reduce(jnp.add, x))
                for fc in range(2):
                    for p in range(2):
                        x = functools.reduce(jnp.add, [column[e] for e in pick[fc, p]])
                        lane = (fr * 2 + fc) * MID
                        row = (q * 2 + p) * LAT
                        w2e[a, row : row + LAT, lane : lane + MID] = x.astype(BF16)

    def prepare(g):
        left = [halo[0, slot, g].astype(F32) for slot in range(3)]
        for t2 in range(2):
            t = 2 * g + t2
            rhs = jnp.concatenate([rc[t].reshape(8 * C, LAT), halo[1, :, g].reshape(48, LAT)], axis=0)
            moved = jnp.dot(sel_ref[t2], rhs, preferred_element_type=F32).astype(BF16)
            for tap in range(9):
                e9[t, :, tap * LAT : (tap + 1) * LAT] = moved[tap * 16 : tap * 16 + 16]
            for row in range(8):
                slot, k = (0, row + 2) if row < 2 else (1, row - 2) if row < 6 else (2, row - 6)
                k = k * 4 + t2 * 2
                x = pltpu.roll(rc[t, row].astype(F32), 1, 0)
                x = jnp.where(row16 == 0, left[slot][k + 1 : k + 2], x)
                m1[t, row] = x.astype(BF16)
                x = jnp.where(row16 == 0, left[slot][k : k + 1], pltpu.roll(x, 1, 0))
                m0[t, row] = x.astype(BF16)

    row16 = lax.broadcasted_iota(jnp.int32, (16, 1), 0)
    top, bottom = r == 0, r == rows - 1
    leftmost, rightmost = c == 0, c == cols - 1

    def shifted_up(x, last):
        return jnp.where(row16 == 15, last, pltpu.roll(x, 15, 0))

    def conv1(f):
        shifts = (m0, m1, rc)
        blocks = []
        for a in range(3):
            for tap, (dr, dc) in enumerate(TAPS):
                x = shifts[dc]
                blocks.append(
                    jnp.concatenate(
                        [x[f + a, dr : dr + 6].reshape(96, LAT), x[f + 1 + a, dr : dr + 6].reshape(96, LAT),
                         e9[f + a, :, tap * LAT : (tap + 1) * LAT], e9[f + 1 + a, :, tap * LAT : (tap + 1) * LAT]],
                        axis=0,
                    )
                )
        lhs = jnp.concatenate(blocks, axis=1)
        total = jnp.dot(lhs, w1[...].reshape(27 * LAT, LAT), preferred_element_type=F32)
        total = jnp.maximum(total, 0.0)
        for i in range(2):
            main = total[i * 96 : i * 96 + 96].reshape(6, 16, LAT)
            edge = total[192 + i * 16 : 208 + i * 16]
            row8 = row16 % 8
            bad = jnp.logical_or(
                jnp.logical_or(jnp.logical_and(row8 == 0, top), jnp.logical_and(row8 == 5, bottom)),
                jnp.logical_and(row16 >= 8, rightmost),
            )
            edge = jnp.where(jnp.logical_or(bad, row8 >= 6), 0.0, edge)
            for q in range(6):
                bad = jnp.logical_and(row16 == 0, leftmost)
                if q == 0:
                    bad = jnp.logical_or(bad, top)
                if q == 5:
                    bad = jnp.logical_or(bad, bottom)
                x = jnp.where(bad, 0.0, main[q])
                f0[f + i, q] = x.astype(BF16)
                f1[f + i, q] = shifted_up(x, edge[q : q + 1]).astype(BF16)
            nothing = jnp.zeros((8, LAT), F32)
            for p in range(2):
                x = edge[p * 8 : p * 8 + 8]
                for q, y in ((0, x), (1, pltpu.roll(x, 7, 0))):
                    lane = (q * 2 + p) * LAT
                    e2[f + i, :, lane : lane + LAT] = jnp.concatenate([y, nothing], axis=0).astype(BF16)

    def conv2(f):
        shifts = (f0, f1)
        blocks = []
        for a in range(3):
            for q in range(2):
                for p in range(2):
                    x = shifts[p]
                    lane = (q * 2 + p) * LAT
                    blocks.append(
                        jnp.concatenate(
                            [x[f + a, q : q + 5].reshape(80, LAT), x[f + 1 + a, q : q + 5].reshape(80, LAT),
                             e2[f + a, :, lane : lane + LAT], e2[f + 1 + a, :, lane : lane + LAT]],
                            axis=0,
                        )
                    )
        lhs = jnp.concatenate(blocks, axis=1)
        total = jnp.dot(lhs, w2e[...].reshape(12 * LAT, 4 * MID), preferred_element_type=F32)
        total = jnp.maximum(total, 0.0)
        for i in range(2):
            for lane in range(4):
                fr, fc = lane // 2, lane % 2
                cut = slice(lane * MID, (lane + 1) * MID)
                edge = total[160 + i * 16 : 176 + i * 16, cut]
                bad = jnp.logical_and(row16 == (0 if fr == 0 else 4), top if fr == 0 else bottom)
                if fc == 1:
                    bad = jnp.logical_or(bad, rightmost)
                edge = jnp.where(bad, 0.0, edge)
                for q in range(5):
                    x = total[i * 80 + q * 16 : i * 80 + q * 16 + 16, cut]
                    if fc == 0:
                        x = jnp.where(jnp.logical_and(row16 == 0, leftmost), 0.0, x)
                    if fr == 0 and q == 0:
                        x = jnp.where(top, 0.0, x)
                    if fr == 1 and q == 4:
                        x = jnp.where(bottom, 0.0, x)
                    s0[f + i, q, :, cut] = x.astype(BF16)
                    s1[f + i, q, :, cut] = shifted_up(x, edge[q : q + 1]).astype(BF16)

    def conv3(f):
        shifts = (s0, s1)
        blocks = []
        for a in range(3):
            for p in range(2):
                for b in range(3):
                    parts = []
                    for parity in range(2):
                        q, fr = divmod(b + parity, 2)
                        for i in range(2):
                            x = shifts[p][f + i + a, q : q + 4, :, fr * 256 : fr * 256 + 256]
                            parts.append(x.reshape(64, 256))
                    blocks.append(jnp.concatenate(parts, axis=0))
        lhs = jnp.concatenate(blocks, axis=1)
        total = jnp.dot(lhs, w3e[...].reshape(18 * 256, 256), preferred_element_type=F32)
        for parity in range(2):
            for i in range(2):
                for q in range(4):
                    at = parity * 128 + i * 64 + q * 16
                    for fc in range(2):
                        woven[fc::2] = total[at : at + 16, fc * MID : (fc + 1) * MID]
                    out_ref[f + i, 2 * q + parity] = woven[...].astype(BF16)

    @pl.when(s > 0)
    def _():
        onward(0).wait_recv()

        @pl.when(s < sections - 1)
        def _():
            onward(2).start()

        spatial_start("B1")

    sel_copy.wait()
    spatial_wait_recv("A")

    @pl.loop(0, 4)
    def _(i):
        f = 6 - 2 * i

        @pl.when(jnp.logical_and(i == 1, s > 0))
        def _():
            onward(1).wait_recv()
            spatial_start("B0")
            spatial_wait_recv("B1")

        @pl.when(jnp.logical_and(i == 2, s > 1))
        def _():
            onward(2).wait_recv()
            spatial_start("C")

        @pl.when(jnp.logical_and(i == 2, s > 0))
        def _():
            spatial_wait_recv("B0")

        @pl.when(jnp.logical_and(i == 3, s > 1))
        def _():
            spatial_wait_recv("C")

        @pl.loop(jnp.where(i == 0, 0, 1), 2)
        def _(k):
            prepare(4 - i - k)

        @pl.when(i == 0)
        def _():
            first_copy.wait()

        conv1(f)

        @pl.when(i >= 1)
        def _():
            conv2(f)

        @pl.when(i == 2)
        def _():
            for copy in third_copies:
                copy.wait()

        @pl.when(i >= 2)
        def _():
            conv3(f)


    spatial_wait_send("A")

    @pl.when(s < sections - 1)
    def _():
        onward(0).wait_send()
        onward(1).wait_send()

    @pl.when(s > 0)
    def _():
        spatial_wait_send("B1")
        spatial_wait_send("B0")

        @pl.when(s < sections - 1)
        def _():
            onward(2).wait_send()

    @pl.when(s > 1)
    def _():
        spatial_wait_send("C")


def solution(mesh):
    sizes = tuple(mesh.shape[a] for a in ("section", "row", "col"))
    sel, pack = selections()

    def per_device(latent, w_first, w_second, w_third):
        hbm = pl.BlockSpec(memory_space=pltpu.HBM)
        vmem = pl.BlockSpec(memory_space=pltpu.VMEM)
        out = pl.pallas_call(
            functools.partial(kernel, sizes),
            out_shape=pltpu.VMEM((T, 2 * R, 2 * C, MID), BF16),
            in_specs=[hbm] * 6,
            out_specs=vmem,
            scratch_shapes=[
                pltpu.VMEM((10, 8, C, LAT), BF16),
                pltpu.VMEM((2, 3, 5, 16, LAT), BF16),
                pltpu.VMEM((2, 5, 16, LAT), BF16),
                pltpu.VMEM((10, 8, C, LAT), BF16),
                pltpu.VMEM((10, 8, C, LAT), BF16),
                pltpu.VMEM((10, 16, 9 * LAT), BF16),
                pltpu.VMEM((8, 6, 16, LAT), BF16),
                pltpu.VMEM((8, 6, 16, LAT), BF16),
                pltpu.VMEM((8, 16, 4 * LAT), BF16),
                pltpu.VMEM((6, 5, 16, 4 * MID), BF16),
                pltpu.VMEM((6, 5, 16, 4 * MID), BF16),
                pltpu.VMEM((3, 3, 3, LAT, LAT), BF16),
                pltpu.VMEM((3, 3, 3, LAT, MID), BF16),
                pltpu.VMEM((3, 4 * LAT, 4 * MID), BF16),
                pltpu.VMEM((3, 2, 3, 2 * MID, 2 * MID), BF16),
                pltpu.VMEM((2, 144, 176), BF16),
                pltpu.VMEM((32, 2 * R * C), BF16),
                pltpu.VMEM((2 * C, MID), F32),
                pltpu.SemaphoreType.DMA((4, 8)),
                pltpu.SemaphoreType.DMA((4, 8)),
                pltpu.SemaphoreType.DMA((3,)),
                pltpu.SemaphoreType.DMA((3,)),
                pltpu.SemaphoreType.DMA((11,)),
            ],
            compiler_params=pltpu.CompilerParams(
                collective_id=0, has_side_effects=True, vmem_limit_bytes=56 * 1024 * 1024
            ),
            cost_estimate=pl.CostEstimate(flops=7 * 10**9, bytes_accessed=8 * 10**6, transcendentals=0),
            name="decoder_block",
        )(latent, w_first, w_second, w_third, jnp.asarray(sel), jnp.asarray(pack))
        return out

    spec = P("section", "row", "col", None)
    return jax.shard_map(
        per_device, mesh=mesh, in_specs=(spec, P(), P(), P()), out_specs=spec, check_vma=False
    )
```

```python
import functools

import jax
import jax.numpy as jnp
import numpy as np
from jax import lax
from jax.experimental import pallas as pl
from jax.experimental.pallas import tpu as pltpu
from jax.sharding import PartitionSpec as P

MESH = pl.DeviceIdType.MESH
BF16 = jnp.bfloat16
F32 = jnp.float32

T, R, C = 4, 4, 16
LAT, MID = 256, 128
DIRS = [(-1, 0), (1, 0), (-1, -1), (-1, 1), (1, -1), (1, 1), (0, -1), (0, 1)]
GROUPS = {"A": (3, 5), "B1": (2, 3), "B0": (1, 2), "C": (0, 1)}
ORDER = {"A": 0, "B1": 1, "B0": 2, "C": 3}
TAPS = [(dr, dc) for dr in range(3) for dc in range(3)]


def selections():
    sel = np.zeros((2, 144, 176), np.float32)

    def source(t2, row, col):
        if col < 18:
            return row * C + col - 2
        slot, r = (0, row + 2) if row < 2 else (1, row - 2) if row < 6 else (2, row - 6)
        return 128 + slot * 16 + r * 4 + t2 * 2 + col - 18

    for t2 in range(2):
        for tap, (dr, dc) in enumerate(TAPS):
            for j in range(2):
                for r in range(6):
                    sel[t2, tap * 16 + j * 8 + r, source(t2, r + dr, 16 + j + dc)] = 1
    pack = np.zeros((32, 128), np.float32)
    for side in range(2):
        for r in range(R):
            for t2 in range(2):
                for c in range(2):
                    pack[side * 16 + r * 4 + t2 * 2 + c, t2 * 64 + r * C + c + 14 * side] = 1
    return sel.astype(jnp.bfloat16), pack.astype(jnp.bfloat16)


def kernel(
    sizes, latent, w1_hbm, w2_hbm, w3_hbm, sel_hbm, pick_hbm, out_ref,
    rc, halo, pack, m0, m1, e9, f0, f1, e2, s0, s1, w1, w2, w2e, w3e, sel_ref, pick_ref, woven,
    send, recv, ysend, yrecv, local,
):
    sections, rows, cols = sizes
    s, r, c = (lax.axis_index(a) for a in ("section", "row", "col"))

    def device(ds, dr, dc):
        return (
            lax.rem(s + ds + sections, sections),
            lax.rem(r + dr + rows, rows),
            lax.rem(c + dc + cols, cols),
        )

    def inside(i, size):
        return jnp.logical_and(i >= 0, i < size)

    def spatial(group, k):
        dr, dc = DIRS[k]
        g0, g1 = GROUPS[group]
        n = ORDER[group]
        if dc == 0:
            src = rc.at[2 * g0 : 2 * g1, pl.ds(4 if dr == 1 else 2, 2)]
            dst = rc.at[2 * g0 : 2 * g1, pl.ds(0 if dr == 1 else 6, 2)]
        else:
            side = 1 if dc == 1 else 0
            src = pack.at[side, g0:g1]
            dst = halo.at[1 - side, 1 - dr, g0:g1]
        return pltpu.make_async_remote_copy(
            src_ref=src, dst_ref=dst, send_sem=send.at[n, k], recv_sem=recv.at[n, k],
            device_id=device(0, dr, dc), device_id_type=MESH,
        )

    def sends(k):
        dr, dc = DIRS[k]
        return jnp.logical_and(inside(r + dr, rows), inside(c + dc, cols))

    def receives(k):
        dr, dc = DIRS[k]
        return jnp.logical_and(inside(r - dr, rows), inside(c - dc, cols))

    def spatial_start(group):
        for k in range(8):
            if k == 2 and group != "A":
                make_pack(GROUPS[group][0])

            @pl.when(sends(k))
            def _():
                spatial(group, k).start()

    def spatial_wait_recv(group):
        for k in range(8):
            @pl.when(receives(k))
            def _():
                spatial(group, k).wait_recv()

    def spatial_wait_send(group):
        for k in range(8):
            @pl.when(sends(k))
            def _():
                spatial(group, k).wait_send()

    def onward(n):
        src, dst = ((8, 4), (6, 2), (4, 0))[n]
        return pltpu.make_async_remote_copy(
            src_ref=rc.at[pl.ds(src, 2), 2:6], dst_ref=rc.at[pl.ds(dst, 2), 2:6],
            send_sem=ysend.at[n], recv_sem=yrecv.at[n],
            device_id=device(1, 0, 0), device_id_type=MESH,
        )

    def make_pack(g):
        own = rc[2 * g : 2 * g + 2, 2:6].reshape(2 * R * C, LAT)
        both = jnp.dot(pick_ref[...], own, preferred_element_type=F32).astype(BF16)
        pack[0, g] = both[0:16]
        pack[1, g] = both[16:32]

    barrier = pltpu.get_barrier_semaphore()
    partners = [(-1, 0, 0)] + [(0, dr, dc) for dr, dc in DIRS] + [(1, 0, 0)]
    for d in partners:
        pl.semaphore_signal(barrier, inc=1, device_id=device(*d), device_id_type=MESH)

    tile = pltpu.make_async_copy(latent, rc.at[6:10, 2:6], local.at[0])
    tile.start()
    sel_copy = pltpu.make_async_copy(sel_hbm, sel_ref, local.at[10])
    sel_copy.start()
    pick_copy = pltpu.make_async_copy(pick_hbm, pick_ref, local.at[9])
    pick_copy.start()
    second_copy = pltpu.make_async_copy(w2_hbm, w2, local.at[1])
    second_copy.start()
    first_copy = pltpu.make_async_copy(w1_hbm, w1, local.at[2])
    first_copy.start()
    third_copies = []
    for n, (e, p, fi, fo) in enumerate(
        [(0, 0, 0, 0), (1, 0, 1, 0), (0, 0, 1, 1), (2, 1, 0, 0), (1, 1, 0, 1), (2, 1, 1, 1)]
    ):
        copy = pltpu.make_async_copy(
            w3_hbm.at[:, :, e],
            w3e.at[:, p, :, fi * MID : (fi + 1) * MID, fo * MID : (fo + 1) * MID],
            local.at[3 + n],
        )
        copy.start()
        third_copies.append(copy)

    tile.wait()
    pick_copy.wait()
    make_pack(4)
    make_pack(3)
    pl.semaphore_wait(barrier, len(partners))

    @pl.when(s < sections - 1)
    def _():
        onward(0).start()

    spatial_start("A")

    @pl.when(s < sections - 1)
    def _():
        onward(1).start()

    @pl.when(r == 0)
    def _():
        rc[:, 0:2] = jnp.zeros((10, 2, C, LAT), BF16)
        halo[:, 0] = jnp.zeros((2, 5, 16, LAT), BF16)

    @pl.when(r == rows - 1)
    def _():
        rc[:, 6:8] = jnp.zeros((10, 2, C, LAT), BF16)
        halo[:, 2] = jnp.zeros((2, 5, 16, LAT), BF16)

    @pl.when(c == 0)
    def _():
        halo[0] = jnp.zeros((3, 5, 16, LAT), BF16)

    @pl.when(c == cols - 1)
    def _():
        halo[1] = jnp.zeros((3, 5, 16, LAT), BF16)

    @pl.when(s == 0)
    def _():
        rc[2:6] = jnp.zeros((4, 8, C, LAT), BF16)
        halo[:, :, 1:3] = jnp.zeros((2, 3, 2, 16, LAT), BF16)

    @pl.when(s <= 1)
    def _():
        rc[0:2] = jnp.zeros((2, 8, C, LAT), BF16)
        halo[:, :, 0:1] = jnp.zeros((2, 3, 1, 16, LAT), BF16)

    w3e[:, 0, :, 0:MID, MID:] = jnp.zeros((3, 3, MID, MID), BF16)
    w3e[:, 1, :, MID:, 0:MID] = jnp.zeros((3, 3, MID, MID), BF16)

    second_copy.wait()
    pick = {(0, 0): (0, 1), (0, 1): (2,), (1, 0): (0,), (1, 1): (1, 2)}

    @pl.loop(0, 3)
    def _(a):
        for fr in range(2):
            for q in range(2):
                column = []
                for e in range(3):
                    x = [w2[a, b, e].astype(F32) for b in pick[fr, q]]
                    column.append(functools.reduce(jnp.add, x))
                for fc in range(2):
                    for p in range(2):
                        x = functools.reduce(jnp.add, [column[e] for e in pick[fc, p]])
                        lane = (fr * 2 + fc) * MID
                        row = (q * 2 + p) * LAT
                        w2e[a, row : row + LAT, lane : lane + MID] = x.astype(BF16)

    def prepare(g):
        left = [halo[0, slot, g].astype(F32) for slot in range(3)]
        for t2 in range(2):
            t = 2 * g + t2
            rhs = jnp.concatenate([rc[t].reshape(8 * C, LAT), halo[1, :, g].reshape(48, LAT)], axis=0)
            moved = jnp.dot(sel_ref[t2], rhs, preferred_element_type=F32).astype(BF16)
            for tap in range(9):
                e9[t, :, tap * LAT : (tap + 1) * LAT] = moved[tap * 16 : tap * 16 + 16]
            for row in range(8):
                slot, k = (0, row + 2) if row < 2 else (1, row - 2) if row < 6 else (2, row - 6)
                k = k * 4 + t2 * 2
                x = pltpu.roll(rc[t, row].astype(F32), 1, 0)
                x = jnp.where(row16 == 0, left[slot][k + 1 : k + 2], x)
                m1[t, row] = x.astype(BF16)
                x = jnp.where(row16 == 0, left[slot][k : k + 1], pltpu.roll(x, 1, 0))
                m0[t, row] = x.astype(BF16)

    row16 = lax.broadcasted_iota(jnp.int32, (16, 1), 0)
    top, bottom = r == 0, r == rows - 1
    leftmost, rightmost = c == 0, c == cols - 1

    def shifted_up(x, last):
        return jnp.where(row16 == 15, last, pltpu.roll(x, 15, 0))

    def conv1(f):
        shifts = (m0, m1, rc)
        blocks = []
        for a in range(3):
            for tap, (dr, dc) in enumerate(TAPS):
                x = shifts[dc]
                blocks.append(
                    jnp.concatenate(
                        [x[f + a, dr : dr + 6].reshape(96, LAT), x[f + 1 + a, dr : dr + 6].reshape(96, LAT),
                         e9[f + a, :, tap * LAT : (tap + 1) * LAT], e9[f + 1 + a, :, tap * LAT : (tap + 1) * LAT]],
                        axis=0,
                    )
                )
        lhs = jnp.concatenate(blocks, axis=1)
        total = jnp.dot(lhs, w1[...].reshape(27 * LAT, LAT), preferred_element_type=F32)
        total = jnp.maximum(total, 0.0)
        for i in range(2):
            main = total[i * 96 : i * 96 + 96].reshape(6, 16, LAT)
            edge = total[192 + i * 16 : 208 + i * 16]
            row8 = row16 % 8
            bad = jnp.logical_or(
                jnp.logical_or(jnp.logical_and(row8 == 0, top), jnp.logical_and(row8 == 5, bottom)),
                jnp.logical_and(row16 >= 8, rightmost),
            )
            edge = jnp.where(jnp.logical_or(bad, row8 >= 6), 0.0, edge)
            for q in range(6):
                bad = jnp.logical_and(row16 == 0, leftmost)
                if q == 0:
                    bad = jnp.logical_or(bad, top)
                if q == 5:
                    bad = jnp.logical_or(bad, bottom)
                x = jnp.where(bad, 0.0, main[q])
                f0[f + i, q] = x.astype(BF16)
                f1[f + i, q] = shifted_up(x, edge[q : q + 1]).astype(BF16)
            nothing = jnp.zeros((8, LAT), F32)
            for p in range(2):
                x = edge[p * 8 : p * 8 + 8]
                for q, y in ((0, x), (1, pltpu.roll(x, 7, 0))):
                    lane = (q * 2 + p) * LAT
                    e2[f + i, :, lane : lane + LAT] = jnp.concatenate([y, nothing], axis=0).astype(BF16)

    def conv2(f):
        shifts = (f0, f1)
        blocks = []
        for a in range(3):
            for q in range(2):
                for p in range(2):
                    x = shifts[p]
                    lane = (q * 2 + p) * LAT
                    blocks.append(
                        jnp.concatenate(
                            [x[f + a, q : q + 5].reshape(80, LAT), x[f + 1 + a, q : q + 5].reshape(80, LAT),
                             e2[f + a, :, lane : lane + LAT], e2[f + 1 + a, :, lane : lane + LAT]],
                            axis=0,
                        )
                    )
        lhs = jnp.concatenate(blocks, axis=1)
        total = jnp.dot(lhs, w2e[...].reshape(12 * LAT, 4 * MID), preferred_element_type=F32)
        total = jnp.maximum(total, 0.0)
        for i in range(2):
            for lane in range(4):
                fr, fc = lane // 2, lane % 2
                cut = slice(lane * MID, (lane + 1) * MID)
                edge = total[160 + i * 16 : 176 + i * 16, cut]
                bad = jnp.logical_and(row16 == (0 if fr == 0 else 4), top if fr == 0 else bottom)
                if fc == 1:
                    bad = jnp.logical_or(bad, rightmost)
                edge = jnp.where(bad, 0.0, edge)
                for q in range(5):
                    x = total[i * 80 + q * 16 : i * 80 + q * 16 + 16, cut]
                    if fc == 0:
                        x = jnp.where(jnp.logical_and(row16 == 0, leftmost), 0.0, x)
                    if fr == 0 and q == 0:
                        x = jnp.where(top, 0.0, x)
                    if fr == 1 and q == 4:
                        x = jnp.where(bottom, 0.0, x)
                    s0[f + i, q, :, cut] = x.astype(BF16)
                    s1[f + i, q, :, cut] = shifted_up(x, edge[q : q + 1]).astype(BF16)

    def conv3(f):
        shifts = (s0, s1)
        blocks = []
        for a in range(3):
            for p in range(2):
                for b in range(3):
                    parts = []
                    for parity in range(2):
                        q, fr = divmod(b + parity, 2)
                        for i in range(2):
                            x = shifts[p][f + i + a, q : q + 4, :, fr * 256 : fr * 256 + 256]
                            parts.append(x.reshape(64, 256))
                    blocks.append(jnp.concatenate(parts, axis=0))
        lhs = jnp.concatenate(blocks, axis=1)
        total = jnp.dot(lhs, w3e[...].reshape(18 * 256, 256), preferred_element_type=F32)
        for parity in range(2):
            for i in range(2):
                for q in range(4):
                    at = parity * 128 + i * 64 + q * 16
                    for fc in range(2):
                        woven[fc::2] = total[at : at + 16, fc * MID : (fc + 1) * MID]
                    out_ref[f + i, 2 * q + parity] = woven[...].astype(BF16)

    @pl.when(s > 0)
    def _():
        onward(0).wait_recv()

        @pl.when(s < sections - 1)
        def _():
            onward(2).start()

        spatial_start("B1")

    sel_copy.wait()
    spatial_wait_recv("A")

    @pl.loop(0, 4)
    def _(i):
        f = 6 - 2 * i

        @pl.when(jnp.logical_and(i == 1, s > 0))
        def _():
            onward(1).wait_recv()
            spatial_start("B0")
            spatial_wait_recv("B1")

        @pl.when(jnp.logical_and(i == 2, s > 0))
        def _():
            spatial_wait_recv("B0")

        @pl.when(jnp.logical_and(i == 3, s > 1))
        def _():
            spatial_wait_recv("C")

        @pl.loop(jnp.where(i == 0, 0, 1), 2)
        def _(k):
            prepare(4 - i - k)

        @pl.when(i == 0)
        def _():
            first_copy.wait()

        conv1(f)

        @pl.when(jnp.logical_and(i == 1, s > 1))
        def _():
            onward(2).wait_recv()
            spatial_start("C")

        @pl.when(i >= 1)
        def _():
            conv2(f)

        @pl.when(i == 2)
        def _():
            for copy in third_copies:
                copy.wait()

        @pl.when(i >= 2)
        def _():
            conv3(f)


    spatial_wait_send("A")

    @pl.when(s < sections - 1)
    def _():
        onward(0).wait_send()
        onward(1).wait_send()

    @pl.when(s > 0)
    def _():
        spatial_wait_send("B1")
        spatial_wait_send("B0")

        @pl.when(s < sections - 1)
        def _():
            onward(2).wait_send()

    @pl.when(s > 1)
    def _():
        spatial_wait_send("C")


def solution(mesh):
    sizes = tuple(mesh.shape[a] for a in ("section", "row", "col"))
    sel, pack = selections()

    def per_device(latent, w_first, w_second, w_third):
        hbm = pl.BlockSpec(memory_space=pltpu.HBM)
        vmem = pl.BlockSpec(memory_space=pltpu.VMEM)
        out = pl.pallas_call(
            functools.partial(kernel, sizes),
            out_shape=pltpu.VMEM((T, 2 * R, 2 * C, MID), BF16),
            in_specs=[hbm] * 6,
            out_specs=vmem,
            scratch_shapes=[
                pltpu.VMEM((10, 8, C, LAT), BF16),
                pltpu.VMEM((2, 3, 5, 16, LAT), BF16),
                pltpu.VMEM((2, 5, 16, LAT), BF16),
                pltpu.VMEM((10, 8, C, LAT), BF16),
                pltpu.VMEM((10, 8, C, LAT), BF16),
                pltpu.VMEM((10, 16, 9 * LAT), BF16),
                pltpu.VMEM((8, 6, 16, LAT), BF16),
                pltpu.VMEM((8, 6, 16, LAT), BF16),
                pltpu.VMEM((8, 16, 4 * LAT), BF16),
                pltpu.VMEM((6, 5, 16, 4 * MID), BF16),
                pltpu.VMEM((6, 5, 16, 4 * MID), BF16),
                pltpu.VMEM((3, 3, 3, LAT, LAT), BF16),
                pltpu.VMEM((3, 3, 3, LAT, MID), BF16),
                pltpu.VMEM((3, 4 * LAT, 4 * MID), BF16),
                pltpu.VMEM((3, 2, 3, 2 * MID, 2 * MID), BF16),
                pltpu.VMEM((2, 144, 176), BF16),
                pltpu.VMEM((32, 2 * R * C), BF16),
                pltpu.VMEM((2 * C, MID), F32),
                pltpu.SemaphoreType.DMA((4, 8)),
                pltpu.SemaphoreType.DMA((4, 8)),
                pltpu.SemaphoreType.DMA((3,)),
                pltpu.SemaphoreType.DMA((3,)),
                pltpu.SemaphoreType.DMA((11,)),
            ],
            compiler_params=pltpu.CompilerParams(
                collective_id=0, has_side_effects=True, vmem_limit_bytes=56 * 1024 * 1024
            ),
            cost_estimate=pl.CostEstimate(flops=7 * 10**9, bytes_accessed=8 * 10**6, transcendentals=0),
            name="decoder_block",
        )(latent, w_first, w_second, w_third, jnp.asarray(sel), jnp.asarray(pack))
        return out

    spec = P("section", "row", "col", None)
    return jax.shard_map(
        per_device, mesh=mesh, in_specs=(spec, P(), P(), P()), out_specs=spec, check_vma=False
    )
```

```python
import functools

import jax
import jax.numpy as jnp
import numpy as np
from jax import lax
from jax.experimental import pallas as pl
from jax.experimental.pallas import tpu as pltpu
from jax.sharding import PartitionSpec as P

MESH = pl.DeviceIdType.MESH
BF16 = jnp.bfloat16
F32 = jnp.float32

T, R, C = 4, 4, 16
LAT, MID = 256, 128
DIRS = [(-1, 0), (1, 0), (-1, -1), (-1, 1), (1, -1), (1, 1), (0, -1), (0, 1)]
GROUPS = {"A": (3, 5), "B1": (2, 3), "B0": (1, 2), "C": (0, 1)}
ORDER = {"A": 0, "B1": 1, "B0": 2, "C": 3}
TAPS = [(dr, dc) for dr in range(3) for dc in range(3)]


def selections():
    sel = np.zeros((2, 144, 176), np.float32)

    def source(t2, row, col):
        if col < 18:
            return row * C + col - 2
        slot, r = (0, row + 2) if row < 2 else (1, row - 2) if row < 6 else (2, row - 6)
        return 128 + slot * 16 + r * 4 + t2 * 2 + col - 18

    for t2 in range(2):
        for tap, (dr, dc) in enumerate(TAPS):
            for j in range(2):
                for r in range(6):
                    sel[t2, tap * 16 + j * 8 + r, source(t2, r + dr, 16 + j + dc)] = 1
    return sel.astype(jnp.bfloat16)


def kernel(
    sizes, latent, w1_hbm, w2_hbm, w3_hbm, sel_hbm, out_ref,
    rc, halo, pack, m0, m1, e9, f0, f1, e2, s0, s1, w1, w2, w2e, w3e, sel_ref, woven,
    send, recv, ysend, yrecv, local,
):
    sections, rows, cols = sizes
    s, r, c = (lax.axis_index(a) for a in ("section", "row", "col"))

    def device(ds, dr, dc):
        return (
            lax.rem(s + ds + sections, sections),
            lax.rem(r + dr + rows, rows),
            lax.rem(c + dc + cols, cols),
        )

    def inside(i, size):
        return jnp.logical_and(i >= 0, i < size)

    def spatial(group, k):
        dr, dc = DIRS[k]
        g0, g1 = GROUPS[group]
        n = ORDER[group]
        if dc == 0:
            src = rc.at[2 * g0 : 2 * g1, pl.ds(4 if dr == 1 else 2, 2)]
            dst = rc.at[2 * g0 : 2 * g1, pl.ds(0 if dr == 1 else 6, 2)]
        else:
            side = 1 if dc == 1 else 0
            src = pack.at[side, g0:g1]
            dst = halo.at[1 - side, 1 - dr, g0:g1]
        return pltpu.make_async_remote_copy(
            src_ref=src, dst_ref=dst, send_sem=send.at[n, k], recv_sem=recv.at[n, k],
            device_id=device(0, dr, dc), device_id_type=MESH,
        )

    def sends(k):
        dr, dc = DIRS[k]
        return jnp.logical_and(inside(r + dr, rows), inside(c + dc, cols))

    def receives(k):
        dr, dc = DIRS[k]
        return jnp.logical_and(inside(r - dr, rows), inside(c - dc, cols))

    def spatial_start(group):
        for k in range(8):
            if k == 2 and group != "A":
                make_pack(GROUPS[group][0])

            @pl.when(sends(k))
            def _():
                spatial(group, k).start()

    def spatial_wait_recv(group):
        for k in range(8):
            @pl.when(receives(k))
            def _():
                spatial(group, k).wait_recv()

    def spatial_wait_send(group):
        for k in range(8):
            @pl.when(sends(k))
            def _():
                spatial(group, k).wait_send()

    def onward(n):
        src, dst = ((8, 4), (6, 2), (4, 0))[n]
        return pltpu.make_async_remote_copy(
            src_ref=rc.at[pl.ds(src, 2), 2:6], dst_ref=rc.at[pl.ds(dst, 2), 2:6],
            send_sem=ysend.at[n], recv_sem=yrecv.at[n],
            device_id=device(1, 0, 0), device_id_type=MESH,
        )

    row8 = lax.broadcasted_iota(jnp.int32, (8, 1), 0)

    def make_pack(g):
        halves = [[jnp.zeros((8, LAT), F32)] * 2 for _ in range(2)]
        for q in range(R):
            for t2 in range(2):
                half, at = divmod(q * 4 + t2 * 2, 8)
                x = rc[2 * g + t2, 2 + q].astype(F32)
                here = jnp.logical_and(row8 >= at, row8 < at + 2)
                for side, y in ((0, x[0:8]), (1, x[8:16])):
                    by = (at - 6 * side) % 8
                    if by:
                        y = pltpu.roll(y, by, 0)
                    halves[side][half] = jnp.where(here, y, halves[side][half])
        for side in range(2):
            pack[side, g] = jnp.concatenate(halves[side], axis=0).astype(BF16)

    barrier = pltpu.get_barrier_semaphore()
    partners = [(-1, 0, 0)] + [(0, dr, dc) for dr, dc in DIRS] + [(1, 0, 0)]
    for d in partners:
        pl.semaphore_signal(barrier, inc=1, device_id=device(*d), device_id_type=MESH)

    tile = pltpu.make_async_copy(latent, rc.at[6:10, 2:6], local.at[0])
    tile.start()
    sel_copy = pltpu.make_async_copy(sel_hbm, sel_ref, local.at[9])
    sel_copy.start()
    second_copy = pltpu.make_async_copy(w2_hbm, w2, local.at[1])
    second_copy.start()
    first_copy = pltpu.make_async_copy(w1_hbm, w1, local.at[2])
    first_copy.start()
    third_copies = []
    for n, (e, p, fi, fo) in enumerate(
        [(0, 0, 0, 0), (1, 0, 1, 0), (0, 0, 1, 1), (2, 1, 0, 0), (1, 1, 0, 1), (2, 1, 1, 1)]
    ):
        copy = pltpu.make_async_copy(
            w3_hbm.at[:, :, e],
            w3e.at[:, p, :, fi * MID : (fi + 1) * MID, fo * MID : (fo + 1) * MID],
            local.at[3 + n],
        )
        copy.start()
        third_copies.append(copy)

    tile.wait()
    make_pack(4)
    make_pack(3)
    pl.semaphore_wait(barrier, len(partners))

    @pl.when(s < sections - 1)
    def _():
        onward(0).start()

    spatial_start("A")

    @pl.when(s < sections - 1)
    def _():
        onward(1).start()

    @pl.when(r == 0)
    def _():
        rc[:, 0:2] = jnp.zeros((10, 2, C, LAT), BF16)
        halo[:, 0] = jnp.zeros((2, 5, 16, LAT), BF16)

    @pl.when(r == rows - 1)
    def _():
        rc[:, 6:8] = jnp.zeros((10, 2, C, LAT), BF16)
        halo[:, 2] = jnp.zeros((2, 5, 16, LAT), BF16)

    @pl.when(c == 0)
    def _():
        halo[0] = jnp.zeros((3, 5, 16, LAT), BF16)

    @pl.when(c == cols - 1)
    def _():
        halo[1] = jnp.zeros((3, 5, 16, LAT), BF16)

    @pl.when(s == 0)
    def _():
        rc[2:6] = jnp.zeros((4, 8, C, LAT), BF16)
        halo[:, :, 1:3] = jnp.zeros((2, 3, 2, 16, LAT), BF16)

    @pl.when(s <= 1)
    def _():
        rc[0:2] = jnp.zeros((2, 8, C, LAT), BF16)
        halo[:, :, 0:1] = jnp.zeros((2, 3, 1, 16, LAT), BF16)

    w3e[:, 0, :, 0:MID, MID:] = jnp.zeros((3, 3, MID, MID), BF16)
    w3e[:, 1, :, MID:, 0:MID] = jnp.zeros((3, 3, MID, MID), BF16)

    second_copy.wait()
    pick = {(0, 0): (0, 1), (0, 1): (2,), (1, 0): (0,), (1, 1): (1, 2)}

    @pl.loop(0, 3)
    def _(a):
        for fr in range(2):
            for q in range(2):
                column = []
                for e in range(3):
                    x = [w2[a, b, e].astype(F32) for b in pick[fr, q]]
                    column.append(functools.reduce(jnp.add, x))
                for fc in range(2):
                    for p in range(2):
                        x = functools.reduce(jnp.add, [column[e] for e in pick[fc, p]])
                        lane = (fr * 2 + fc) * MID
                        row = (q * 2 + p) * LAT
                        w2e[a, row : row + LAT, lane : lane + MID] = x.astype(BF16)

    def prepare(g):
        left = [halo[0, slot, g].astype(F32) for slot in range(3)]
        for t2 in range(2):
            t = 2 * g + t2
            rhs = jnp.concatenate([rc[t].reshape(8 * C, LAT), halo[1, :, g].reshape(48, LAT)], axis=0)
            moved = jnp.dot(sel_ref[t2], rhs, preferred_element_type=F32).astype(BF16)
            for tap in range(9):
                e9[t, :, tap * LAT : (tap + 1) * LAT] = moved[tap * 16 : tap * 16 + 16]
            for row in range(8):
                slot, k = (0, row + 2) if row < 2 else (1, row - 2) if row < 6 else (2, row - 6)
                k = k * 4 + t2 * 2
                x = pltpu.roll(rc[t, row].astype(F32), 1, 0)
                x = jnp.where(row16 == 0, left[slot][k + 1 : k + 2], x)
                m1[t, row] = x.astype(BF16)
                x = jnp.where(row16 == 0, left[slot][k : k + 1], pltpu.roll(x, 1, 0))
                m0[t, row] = x.astype(BF16)

    row16 = lax.broadcasted_iota(jnp.int32, (16, 1), 0)
    top, bottom = r == 0, r == rows - 1
    leftmost, rightmost = c == 0, c == cols - 1

    def shifted_up(x, last):
        return jnp.where(row16 == 15, last, pltpu.roll(x, 15, 0))

    def conv1(f):
        shifts = (m0, m1, rc)
        blocks = []
        for a in range(3):
            for tap, (dr, dc) in enumerate(TAPS):
                x = shifts[dc]
                blocks.append(
                    jnp.concatenate(
                        [x[f + a, dr : dr + 6].reshape(96, LAT), x[f + 1 + a, dr : dr + 6].reshape(96, LAT),
                         e9[f + a, :, tap * LAT : (tap + 1) * LAT], e9[f + 1 + a, :, tap * LAT : (tap + 1) * LAT]],
                        axis=0,
                    )
                )
        lhs = jnp.concatenate(blocks, axis=1)
        total = jnp.dot(lhs, w1[...].reshape(27 * LAT, LAT), preferred_element_type=F32)
        total = jnp.maximum(total, 0.0)
        for i in range(2):
            main = total[i * 96 : i * 96 + 96].reshape(6, 16, LAT)
            edge = total[192 + i * 16 : 208 + i * 16]
            row8 = row16 % 8
            bad = jnp.logical_or(
                jnp.logical_or(jnp.logical_and(row8 == 0, top), jnp.logical_and(row8 == 5, bottom)),
                jnp.logical_and(row16 >= 8, rightmost),
            )
            edge = jnp.where(jnp.logical_or(bad, row8 >= 6), 0.0, edge)
            for q in range(6):
                bad = jnp.logical_and(row16 == 0, leftmost)
                if q == 0:
                    bad = jnp.logical_or(bad, top)
                if q == 5:
                    bad = jnp.logical_or(bad, bottom)
                x = jnp.where(bad, 0.0, main[q])
                f0[f + i, q] = x.astype(BF16)
                f1[f + i, q] = shifted_up(x, edge[q : q + 1]).astype(BF16)
            nothing = jnp.zeros((8, LAT), F32)
            for p in range(2):
                x = edge[p * 8 : p * 8 + 8]
                for q, y in ((0, x), (1, pltpu.roll(x, 7, 0))):
                    lane = (q * 2 + p) * LAT
                    e2[f + i, :, lane : lane + LAT] = jnp.concatenate([y, nothing], axis=0).astype(BF16)

    def conv2(f):
        shifts = (f0, f1)
        blocks = []
        for a in range(3):
            for q in range(2):
                for p in range(2):
                    x = shifts[p]
                    lane = (q * 2 + p) * LAT
                    blocks.append(
                        jnp.concatenate(
                            [x[f + a, q : q + 5].reshape(80, LAT), x[f + 1 + a, q : q + 5].reshape(80, LAT),
                             e2[f + a, :, lane : lane + LAT], e2[f + 1 + a, :, lane : lane + LAT]],
                            axis=0,
                        )
                    )
        lhs = jnp.concatenate(blocks, axis=1)
        total = jnp.dot(lhs, w2e[...].reshape(12 * LAT, 4 * MID), preferred_element_type=F32)
        total = jnp.maximum(total, 0.0)
        for i in range(2):
            for lane in range(4):
                fr, fc = lane // 2, lane % 2
                cut = slice(lane * MID, (lane + 1) * MID)
                edge = total[160 + i * 16 : 176 + i * 16, cut]
                bad = jnp.logical_and(row16 == (0 if fr == 0 else 4), top if fr == 0 else bottom)
                if fc == 1:
                    bad = jnp.logical_or(bad, rightmost)
                edge = jnp.where(bad, 0.0, edge)
                for q in range(5):
                    x = total[i * 80 + q * 16 : i * 80 + q * 16 + 16, cut]
                    if fc == 0:
                        x = jnp.where(jnp.logical_and(row16 == 0, leftmost), 0.0, x)
                    if fr == 0 and q == 0:
                        x = jnp.where(top, 0.0, x)
                    if fr == 1 and q == 4:
                        x = jnp.where(bottom, 0.0, x)
                    s0[f + i, q, :, cut] = x.astype(BF16)
                    s1[f + i, q, :, cut] = shifted_up(x, edge[q : q + 1]).astype(BF16)

    def conv3(f):
        shifts = (s0, s1)
        blocks = []
        for a in range(3):
            for p in range(2):
                for b in range(3):
                    parts = []
                    for parity in range(2):
                        q, fr = divmod(b + parity, 2)
                        for i in range(2):
                            x = shifts[p][f + i + a, q : q + 4, :, fr * 256 : fr * 256 + 256]
                            parts.append(x.reshape(64, 256))
                    blocks.append(jnp.concatenate(parts, axis=0))
        lhs = jnp.concatenate(blocks, axis=1)
        total = jnp.dot(lhs, w3e[...].reshape(18 * 256, 256), preferred_element_type=F32)
        for parity in range(2):
            for i in range(2):
                for q in range(4):
                    at = parity * 128 + i * 64 + q * 16
                    for fc in range(2):
                        woven[fc::2] = total[at : at + 16, fc * MID : (fc + 1) * MID]
                    out_ref[f + i, 2 * q + parity] = woven[...].astype(BF16)

    @pl.when(s > 0)
    def _():
        onward(0).wait_recv()

        @pl.when(s < sections - 1)
        def _():
            onward(2).start()

        spatial_start("B1")

    sel_copy.wait()
    spatial_wait_recv("A")

    @pl.loop(0, 4)
    def _(i):
        f = 6 - 2 * i

        @pl.when(jnp.logical_and(i == 1, s > 0))
        def _():
            onward(1).wait_recv()
            spatial_start("B0")
            spatial_wait_recv("B1")

        @pl.when(jnp.logical_and(i == 2, s > 0))
        def _():
            spatial_wait_recv("B0")

        @pl.when(jnp.logical_and(i == 3, s > 1))
        def _():
            spatial_wait_recv("C")

        @pl.loop(jnp.where(i == 0, 0, 1), 2)
        def _(k):
            prepare(4 - i - k)

        @pl.when(i == 0)
        def _():
            first_copy.wait()

        conv1(f)

        @pl.when(jnp.logical_and(i == 1, s > 1))
        def _():
            onward(2).wait_recv()
            spatial_start("C")

        @pl.when(i >= 1)
        def _():
            conv2(f)

        @pl.when(i == 2)
        def _():
            for copy in third_copies:
                copy.wait()

        @pl.when(i >= 2)
        def _():
            conv3(f)


    spatial_wait_send("A")

    @pl.when(s < sections - 1)
    def _():
        onward(0).wait_send()
        onward(1).wait_send()

    @pl.when(s > 0)
    def _():
        spatial_wait_send("B1")
        spatial_wait_send("B0")

        @pl.when(s < sections - 1)
        def _():
            onward(2).wait_send()

    @pl.when(s > 1)
    def _():
        spatial_wait_send("C")


def solution(mesh):
    sizes = tuple(mesh.shape[a] for a in ("section", "row", "col"))
    sel = selections()

    def per_device(latent, w_first, w_second, w_third):
        hbm = pl.BlockSpec(memory_space=pltpu.HBM)
        vmem = pl.BlockSpec(memory_space=pltpu.VMEM)
        out = pl.pallas_call(
            functools.partial(kernel, sizes),
            out_shape=pltpu.VMEM((T, 2 * R, 2 * C, MID), BF16),
            in_specs=[hbm] * 5,
            out_specs=vmem,
            scratch_shapes=[
                pltpu.VMEM((10, 8, C, LAT), BF16),
                pltpu.VMEM((2, 3, 5, 16, LAT), BF16),
                pltpu.VMEM((2, 5, 16, LAT), BF16),
                pltpu.VMEM((10, 8, C, LAT), BF16),
                pltpu.VMEM((10, 8, C, LAT), BF16),
                pltpu.VMEM((10, 16, 9 * LAT), BF16),
                pltpu.VMEM((8, 6, 16, LAT), BF16),
                pltpu.VMEM((8, 6, 16, LAT), BF16),
                pltpu.VMEM((8, 16, 4 * LAT), BF16),
                pltpu.VMEM((6, 5, 16, 4 * MID), BF16),
                pltpu.VMEM((6, 5, 16, 4 * MID), BF16),
                pltpu.VMEM((3, 3, 3, LAT, LAT), BF16),
                pltpu.VMEM((3, 3, 3, LAT, MID), BF16),
                pltpu.VMEM((3, 4 * LAT, 4 * MID), BF16),
                pltpu.VMEM((3, 2, 3, 2 * MID, 2 * MID), BF16),
                pltpu.VMEM((2, 144, 176), BF16),
                pltpu.VMEM((2 * C, MID), F32),
                pltpu.SemaphoreType.DMA((4, 8)),
                pltpu.SemaphoreType.DMA((4, 8)),
                pltpu.SemaphoreType.DMA((3,)),
                pltpu.SemaphoreType.DMA((3,)),
                pltpu.SemaphoreType.DMA((10,)),
            ],
            compiler_params=pltpu.CompilerParams(
                collective_id=0, has_side_effects=True, vmem_limit_bytes=56 * 1024 * 1024
            ),
            cost_estimate=pl.CostEstimate(flops=7 * 10**9, bytes_accessed=8 * 10**6, transcendentals=0),
            name="decoder_block",
        )(latent, w_first, w_second, w_third, jnp.asarray(sel))
        return out

    spec = P("section", "row", "col", None)
    return jax.shard_map(
        per_device, mesh=mesh, in_specs=(spec, P(), P(), P()), out_specs=spec, check_vma=False
    )
```

```python
import functools

import jax
import jax.numpy as jnp
import numpy as np
from jax import lax
from jax.experimental import pallas as pl
from jax.experimental.pallas import tpu as pltpu
from jax.sharding import PartitionSpec as P

MESH = pl.DeviceIdType.MESH
BF16 = jnp.bfloat16
F32 = jnp.float32

T, R, C = 4, 4, 16
LAT, MID = 256, 128
DIRS = [(-1, 0), (1, 0), (-1, -1), (-1, 1), (1, -1), (1, 1), (0, -1), (0, 1)]
GROUPS = {"A": (3, 5), "B1": (2, 3), "B0": (1, 2), "C": (0, 1)}
ORDER = {"A": 0, "B1": 1, "B0": 2, "C": 3}
TAPS = [(dr, dc) for dr in range(3) for dc in range(3)]


def selections():
    sel = np.zeros((2, 144, 176), np.float32)

    def source(t2, row, col):
        if col < 18:
            return row * C + col - 2
        slot, r = (0, row + 2) if row < 2 else (1, row - 2) if row < 6 else (2, row - 6)
        return 128 + slot * 16 + r * 4 + t2 * 2 + col - 18

    for t2 in range(2):
        for tap, (dr, dc) in enumerate(TAPS):
            for j in range(2):
                for r in range(6):
                    sel[t2, tap * 16 + j * 8 + r, source(t2, r + dr, 16 + j + dc)] = 1
    return sel.astype(jnp.bfloat16)


def kernel(
    sizes, latent, w1_hbm, w2_hbm, w3_hbm, sel_hbm, out_ref,
    rc, halo, pack, m0, m1, e9, f0, f1, e2, s0, s1, w1, w2, w2e, w3e, sel_ref, woven,
    send, recv, ysend, yrecv, local,
):
    sections, rows, cols = sizes
    s, r, c = (lax.axis_index(a) for a in ("section", "row", "col"))

    def device(ds, dr, dc):
        return (
            lax.rem(s + ds + sections, sections),
            lax.rem(r + dr + rows, rows),
            lax.rem(c + dc + cols, cols),
        )

    def inside(i, size):
        return jnp.logical_and(i >= 0, i < size)

    def spatial(group, k):
        dr, dc = DIRS[k]
        g0, g1 = GROUPS[group]
        n = ORDER[group]
        if dc == 0:
            src = rc.at[2 * g0 : 2 * g1, pl.ds(4 if dr == 1 else 2, 2)]
            dst = rc.at[2 * g0 : 2 * g1, pl.ds(0 if dr == 1 else 6, 2)]
        else:
            side = 1 if dc == 1 else 0
            src = pack.at[side, g0:g1]
            dst = halo.at[1 - side, 1 - dr, g0:g1]
        return pltpu.make_async_remote_copy(
            src_ref=src, dst_ref=dst, send_sem=send.at[n, k], recv_sem=recv.at[n, k],
            device_id=device(0, dr, dc), device_id_type=MESH,
        )

    def sends(k):
        dr, dc = DIRS[k]
        return jnp.logical_and(inside(r + dr, rows), inside(c + dc, cols))

    def receives(k):
        dr, dc = DIRS[k]
        return jnp.logical_and(inside(r - dr, rows), inside(c - dc, cols))

    def spatial_start(group):
        for k in range(8):
            if k == 2 and group != "A":
                make_pack(GROUPS[group][0])

            @pl.when(sends(k))
            def _():
                spatial(group, k).start()

    def spatial_wait_recv(group):
        for k in range(8):
            @pl.when(receives(k))
            def _():
                spatial(group, k).wait_recv()

    def spatial_wait_send(group):
        for k in range(8):
            @pl.when(sends(k))
            def _():
                spatial(group, k).wait_send()

    def onward(n):
        src, dst = ((8, 4), (6, 2), (4, 0))[n]
        return pltpu.make_async_remote_copy(
            src_ref=rc.at[pl.ds(src, 2), 2:6], dst_ref=rc.at[pl.ds(dst, 2), 2:6],
            send_sem=ysend.at[n], recv_sem=yrecv.at[n],
            device_id=device(1, 0, 0), device_id_type=MESH,
        )

    row8 = lax.broadcasted_iota(jnp.int32, (8, 1), 0)

    def make_pack(g):
        halves = [[jnp.zeros((8, LAT), F32)] * 2 for _ in range(2)]
        for q in range(R):
            for t2 in range(2):
                half, at = divmod(q * 4 + t2 * 2, 8)
                x = rc[2 * g + t2, 2 + q].astype(F32)
                here = jnp.logical_and(row8 >= at, row8 < at + 2)
                for side, y in ((0, x[0:8]), (1, x[8:16])):
                    by = (at - 6 * side) % 8
                    if by:
                        y = pltpu.roll(y, by, 0)
                    halves[side][half] = jnp.where(here, y, halves[side][half])
        for side in range(2):
            pack[side, g] = jnp.concatenate(halves[side], axis=0).astype(BF16)

    barrier = pltpu.get_barrier_semaphore()
    partners = [(-1, 0, 0)] + [(0, dr, dc) for dr, dc in DIRS] + [(1, 0, 0)]
    for d in partners:
        pl.semaphore_signal(barrier, inc=1, device_id=device(*d), device_id_type=MESH)

    tile = pltpu.make_async_copy(latent, rc.at[6:10, 2:6], local.at[0])
    tile.start()
    sel_copy = pltpu.make_async_copy(sel_hbm, sel_ref, local.at[9])
    sel_copy.start()
    second_copy = pltpu.make_async_copy(w2_hbm, w2, local.at[1])
    second_copy.start()
    first_copy = pltpu.make_async_copy(w1_hbm, w1, local.at[2])
    first_copy.start()
    third_copies = []
    for n, (e, p, fi, fo) in enumerate(
        [(0, 0, 0, 0), (1, 0, 1, 0), (0, 0, 1, 1), (2, 1, 0, 0), (1, 1, 0, 1), (2, 1, 1, 1)]
    ):
        copy = pltpu.make_async_copy(
            w3_hbm.at[:, :, e],
            w3e.at[:, p, :, fi * MID : (fi + 1) * MID, fo * MID : (fo + 1) * MID],
            local.at[3 + n],
        )
        copy.start()
        third_copies.append(copy)

    tile.wait()
    make_pack(4)
    make_pack(3)
    pl.semaphore_wait(barrier, len(partners))

    @pl.when(s < sections - 1)
    def _():
        onward(0).start()

    spatial_start("A")

    @pl.when(s < sections - 1)
    def _():
        onward(1).start()

    @pl.when(r == 0)
    def _():
        rc[:, 0:2] = jnp.zeros((10, 2, C, LAT), BF16)
        halo[:, 0] = jnp.zeros((2, 5, 16, LAT), BF16)

    @pl.when(r == rows - 1)
    def _():
        rc[:, 6:8] = jnp.zeros((10, 2, C, LAT), BF16)
        halo[:, 2] = jnp.zeros((2, 5, 16, LAT), BF16)

    @pl.when(c == 0)
    def _():
        halo[0] = jnp.zeros((3, 5, 16, LAT), BF16)

    @pl.when(c == cols - 1)
    def _():
        halo[1] = jnp.zeros((3, 5, 16, LAT), BF16)

    @pl.when(s == 0)
    def _():
        rc[2:6] = jnp.zeros((4, 8, C, LAT), BF16)
        halo[:, :, 1:3] = jnp.zeros((2, 3, 2, 16, LAT), BF16)

    @pl.when(s <= 1)
    def _():
        rc[0:2] = jnp.zeros((2, 8, C, LAT), BF16)
        halo[:, :, 0:1] = jnp.zeros((2, 3, 1, 16, LAT), BF16)

    w3e[:, 0, :, 0:MID, MID:] = jnp.zeros((3, 3, MID, MID), BF16)
    w3e[:, 1, :, MID:, 0:MID] = jnp.zeros((3, 3, MID, MID), BF16)

    second_copy.wait()
    pick = {(0, 0): (0, 1), (0, 1): (2,), (1, 0): (0,), (1, 1): (1, 2)}

    @pl.loop(0, 3)
    def _(a):
        for fr in range(2):
            for q in range(2):
                column = []
                for e in range(3):
                    x = [w2[a, b, e].astype(F32) for b in pick[fr, q]]
                    column.append(functools.reduce(jnp.add, x))
                for fc in range(2):
                    for p in range(2):
                        x = functools.reduce(jnp.add, [column[e] for e in pick[fc, p]])
                        lane = (fr * 2 + fc) * MID
                        row = (q * 2 + p) * LAT
                        w2e[a, row : row + LAT, lane : lane + MID] = x.astype(BF16)

    def prepare(g):
        left = [halo[0, slot, g].astype(F32) for slot in range(3)]
        for t2 in range(2):
            t = 2 * g + t2
            rhs = jnp.concatenate([rc[t].reshape(8 * C, LAT), halo[1, :, g].reshape(48, LAT)], axis=0)
            moved = jnp.dot(sel_ref[t2], rhs, preferred_element_type=F32).astype(BF16)
            for tap in range(9):
                e9[t, :, tap * LAT : (tap + 1) * LAT] = moved[tap * 16 : tap * 16 + 16]
            for row in range(8):
                slot, k = (0, row + 2) if row < 2 else (1, row - 2) if row < 6 else (2, row - 6)
                k = k * 4 + t2 * 2
                x = pltpu.roll(rc[t, row].astype(F32), 1, 0)
                x = jnp.where(row16 == 0, left[slot][k + 1 : k + 2], x)
                m1[t, row] = x.astype(BF16)
                x = jnp.where(row16 == 0, left[slot][k : k + 1], pltpu.roll(x, 1, 0))
                m0[t, row] = x.astype(BF16)

    row16 = lax.broadcasted_iota(jnp.int32, (16, 1), 0)
    top, bottom = r == 0, r == rows - 1
    leftmost, rightmost = c == 0, c == cols - 1

    def shifted_up(x, last):
        return jnp.where(row16 == 15, last, pltpu.roll(x, 15, 0))

    def conv1(f):
        shifts = (m0, m1, rc)
        blocks = []
        for a in range(3):
            for tap, (dr, dc) in enumerate(TAPS):
                x = shifts[dc]
                blocks.append(
                    jnp.concatenate(
                        [x[f + a, dr : dr + 6].reshape(96, LAT), x[f + 1 + a, dr : dr + 6].reshape(96, LAT),
                         e9[f + a, :, tap * LAT : (tap + 1) * LAT], e9[f + 1 + a, :, tap * LAT : (tap + 1) * LAT]],
                        axis=0,
                    )
                )
        lhs = jnp.concatenate(blocks, axis=1)
        total = jnp.dot(lhs, w1[...].reshape(27 * LAT, LAT), preferred_element_type=F32)
        total = jnp.maximum(total, 0.0)
        for i in range(2):
            main = total[i * 96 : i * 96 + 96].reshape(6, 16, LAT)
            edge = total[192 + i * 16 : 208 + i * 16]
            row8 = row16 % 8
            bad = jnp.logical_or(
                jnp.logical_or(jnp.logical_and(row8 == 0, top), jnp.logical_and(row8 == 5, bottom)),
                jnp.logical_and(row16 >= 8, rightmost),
            )
            edge = jnp.where(jnp.logical_or(bad, row8 >= 6), 0.0, edge)
            for q in range(6):
                bad = jnp.logical_and(row16 == 0, leftmost)
                if q == 0:
                    bad = jnp.logical_or(bad, top)
                if q == 5:
                    bad = jnp.logical_or(bad, bottom)
                x = jnp.where(bad, 0.0, main[q])
                f0[f + i, q] = x.astype(BF16)
                f1[f + i, q] = shifted_up(x, edge[q : q + 1]).astype(BF16)
            nothing = jnp.zeros((8, LAT), F32)
            for p in range(2):
                x = edge[p * 8 : p * 8 + 8]
                for q, y in ((0, x), (1, pltpu.roll(x, 7, 0))):
                    lane = (q * 2 + p) * LAT
                    e2[f + i, :, lane : lane + LAT] = jnp.concatenate([y, nothing], axis=0).astype(BF16)

    def conv2(f):
        shifts = (f0, f1)
        blocks = []
        for a in range(3):
            for q in range(2):
                for p in range(2):
                    x = shifts[p]
                    lane = (q * 2 + p) * LAT
                    blocks.append(
                        jnp.concatenate(
                            [x[f + a, q : q + 5].reshape(80, LAT), x[f + 1 + a, q : q + 5].reshape(80, LAT),
                             e2[f + a, :, lane : lane + LAT], e2[f + 1 + a, :, lane : lane + LAT]],
                            axis=0,
                        )
                    )
        lhs = jnp.concatenate(blocks, axis=1)
        total = jnp.dot(lhs, w2e[...].reshape(12 * LAT, 4 * MID), preferred_element_type=F32)
        total = jnp.maximum(total, 0.0)
        for i in range(2):
            for lane in range(4):
                fr, fc = lane // 2, lane % 2
                cut = slice(lane * MID, (lane + 1) * MID)
                edge = total[160 + i * 16 : 176 + i * 16, cut]
                bad = jnp.logical_and(row16 == (0 if fr == 0 else 4), top if fr == 0 else bottom)
                if fc == 1:
                    bad = jnp.logical_or(bad, rightmost)
                edge = jnp.where(bad, 0.0, edge)
                for q in range(5):
                    x = total[i * 80 + q * 16 : i * 80 + q * 16 + 16, cut]
                    if fc == 0:
                        x = jnp.where(jnp.logical_and(row16 == 0, leftmost), 0.0, x)
                    if fr == 0 and q == 0:
                        x = jnp.where(top, 0.0, x)
                    if fr == 1 and q == 4:
                        x = jnp.where(bottom, 0.0, x)
                    s0[f + i, q, :, cut] = x.astype(BF16)
                    s1[f + i, q, :, cut] = shifted_up(x, edge[q : q + 1]).astype(BF16)

    def conv3(f):
        shifts = (s0, s1)
        blocks = []
        for a in range(3):
            for p in range(2):
                for b in range(3):
                    parts = []
                    for parity in range(2):
                        q, fr = divmod(b + parity, 2)
                        for i in range(2):
                            x = shifts[p][f + i + a, q : q + 4, :, fr * 256 : fr * 256 + 256]
                            parts.append(x.reshape(64, 256))
                    blocks.append(jnp.concatenate(parts, axis=0))
        lhs = jnp.concatenate(blocks, axis=1)
        total = jnp.dot(lhs, w3e[...].reshape(18 * 256, 256), preferred_element_type=F32)
        for parity in range(2):
            for i in range(2):
                for q in range(4):
                    at = parity * 128 + i * 64 + q * 16
                    for fc in range(2):
                        woven[fc::2] = total[at : at + 16, fc * MID : (fc + 1) * MID]
                    out_ref[f + i, 2 * q + parity] = woven[...].astype(BF16)

    @pl.when(s > 0)
    def _():
        onward(0).wait_recv()

        @pl.when(s < sections - 1)
        def _():
            onward(2).start()

        spatial_start("B1")

    sel_copy.wait()
    spatial_wait_recv("A")

    @pl.loop(0, 4)
    def _(i):
        f = 6 - 2 * i

        @pl.when(jnp.logical_and(i == 1, s > 0))
        def _():
            onward(1).wait_recv()
            spatial_start("B0")

        @pl.when(i == 1)
        def _():
            spatial_wait_send("A")

        @pl.when(jnp.logical_and(i == 1, s < sections - 1))
        def _():
            onward(0).wait_send()
            onward(1).wait_send()

        @pl.when(jnp.logical_and(i == 1, s > 0))
        def _():
            spatial_wait_recv("B1")

        @pl.when(jnp.logical_and(i == 2, s > 0))
        def _():
            spatial_wait_recv("B0")

        @pl.when(jnp.logical_and(i == 3, s > 0))
        def _():
            spatial_wait_send("B1")
            spatial_wait_send("B0")

            @pl.when(s < sections - 1)
            def _():
                onward(2).wait_send()

        @pl.when(jnp.logical_and(i == 3, s > 1))
        def _():
            spatial_wait_send("C")
            spatial_wait_recv("C")

        @pl.loop(jnp.where(i == 0, 0, 1), 2)
        def _(k):
            prepare(4 - i - k)

        @pl.when(i == 0)
        def _():
            first_copy.wait()

        conv1(f)

        @pl.when(jnp.logical_and(i == 1, s > 1))
        def _():
            onward(2).wait_recv()
            spatial_start("C")

        @pl.when(i >= 1)
        def _():
            conv2(f)

        @pl.when(i == 2)
        def _():
            for copy in third_copies:
                copy.wait()

        @pl.when(i >= 2)
        def _():
            conv3(f)


def solution(mesh):
    sizes = tuple(mesh.shape[a] for a in ("section", "row", "col"))
    sel = selections()

    def per_device(latent, w_first, w_second, w_third):
        hbm = pl.BlockSpec(memory_space=pltpu.HBM)
        vmem = pl.BlockSpec(memory_space=pltpu.VMEM)
        out = pl.pallas_call(
            functools.partial(kernel, sizes),
            out_shape=pltpu.VMEM((T, 2 * R, 2 * C, MID), BF16),
            in_specs=[hbm] * 5,
            out_specs=vmem,
            scratch_shapes=[
                pltpu.VMEM((10, 8, C, LAT), BF16),
                pltpu.VMEM((2, 3, 5, 16, LAT), BF16),
                pltpu.VMEM((2, 5, 16, LAT), BF16),
                pltpu.VMEM((10, 8, C, LAT), BF16),
                pltpu.VMEM((10, 8, C, LAT), BF16),
                pltpu.VMEM((10, 16, 9 * LAT), BF16),
                pltpu.VMEM((8, 6, 16, LAT), BF16),
                pltpu.VMEM((8, 6, 16, LAT), BF16),
                pltpu.VMEM((8, 16, 4 * LAT), BF16),
                pltpu.VMEM((6, 5, 16, 4 * MID), BF16),
                pltpu.VMEM((6, 5, 16, 4 * MID), BF16),
                pltpu.VMEM((3, 3, 3, LAT, LAT), BF16),
                pltpu.VMEM((3, 3, 3, LAT, MID), BF16),
                pltpu.VMEM((3, 4 * LAT, 4 * MID), BF16),
                pltpu.VMEM((3, 2, 3, 2 * MID, 2 * MID), BF16),
                pltpu.VMEM((2, 144, 176), BF16),
                pltpu.VMEM((2 * C, MID), F32),
                pltpu.SemaphoreType.DMA((4, 8)),
                pltpu.SemaphoreType.DMA((4, 8)),
                pltpu.SemaphoreType.DMA((3,)),
                pltpu.SemaphoreType.DMA((3,)),
                pltpu.SemaphoreType.DMA((10,)),
            ],
            compiler_params=pltpu.CompilerParams(
                collective_id=0, has_side_effects=True, vmem_limit_bytes=56 * 1024 * 1024
            ),
            cost_estimate=pl.CostEstimate(flops=7 * 10**9, bytes_accessed=8 * 10**6, transcendentals=0),
            name="decoder_block",
        )(latent, w_first, w_second, w_third, jnp.asarray(sel))
        return out

    spec = P("section", "row", "col", None)
    return jax.shard_map(
        per_device, mesh=mesh, in_specs=(spec, P(), P(), P()), out_specs=spec, check_vma=False
    )
```

```python
import functools

import jax
import jax.numpy as jnp
import numpy as np
from jax import lax
from jax.experimental import pallas as pl
from jax.experimental.pallas import tpu as pltpu
from jax.sharding import PartitionSpec as P

MESH = pl.DeviceIdType.MESH
BF16 = jnp.bfloat16
F32 = jnp.float32

T, R, C = 4, 4, 16
LAT, MID = 256, 128
DIRS = [(-1, 0), (1, 0), (-1, -1), (-1, 1), (1, -1), (1, 1), (0, -1), (0, 1)]
GROUPS = {"A": (3, 5), "B1": (2, 3), "B0": (1, 2), "C": (0, 1)}
ORDER = {"A": 0, "B1": 1, "B0": 2, "C": 3}
TAPS = [(dr, dc) for dr in range(3) for dc in range(3)]


def selections():
    sel = np.zeros((2, 144, 176), np.float32)

    def source(t2, row, col):
        if col < 18:
            return row * C + col - 2
        slot, r = (0, row + 2) if row < 2 else (1, row - 2) if row < 6 else (2, row - 6)
        return 128 + slot * 16 + r * 4 + t2 * 2 + col - 18

    for t2 in range(2):
        for tap, (dr, dc) in enumerate(TAPS):
            for j in range(2):
                for r in range(6):
                    sel[t2, tap * 16 + j * 8 + r, source(t2, r + dr, 16 + j + dc)] = 1
    return sel.astype(jnp.bfloat16)


def kernel(
    sizes, latent, w1_hbm, w2_hbm, w3_hbm, sel_hbm, out_ref,
    rc, halo, pack, m0, m1, e9, f0, f1, e2, s0, s1, w1, w2, w2e, w3e, sel_ref, woven,
    send, recv, ysend, yrecv, local,
):
    sections, rows, cols = sizes
    s, r, c = (lax.axis_index(a) for a in ("section", "row", "col"))

    def device(ds, dr, dc):
        return (
            lax.rem(s + ds + sections, sections),
            lax.rem(r + dr + rows, rows),
            lax.rem(c + dc + cols, cols),
        )

    def inside(i, size):
        return jnp.logical_and(i >= 0, i < size)

    def spatial(group, k):
        dr, dc = DIRS[k]
        g0, g1 = GROUPS[group]
        n = ORDER[group]
        if dc == 0:
            src = rc.at[2 * g0 : 2 * g1, pl.ds(4 if dr == 1 else 2, 2)]
            dst = rc.at[2 * g0 : 2 * g1, pl.ds(0 if dr == 1 else 6, 2)]
        else:
            side = 1 if dc == 1 else 0
            src = pack.at[side, g0:g1]
            dst = halo.at[1 - side, 1 - dr, g0:g1]
        return pltpu.make_async_remote_copy(
            src_ref=src, dst_ref=dst, send_sem=send.at[n, k], recv_sem=recv.at[n, k],
            device_id=device(0, dr, dc), device_id_type=MESH,
        )

    def sends(k):
        dr, dc = DIRS[k]
        return jnp.logical_and(inside(r + dr, rows), inside(c + dc, cols))

    def receives(k):
        dr, dc = DIRS[k]
        return jnp.logical_and(inside(r - dr, rows), inside(c - dc, cols))

    interior = jnp.logical_and(
        jnp.logical_and(r > 0, r < rows - 1), jnp.logical_and(c > 0, c < cols - 1)
    )

    def each(ks, condition, action):
        @pl.when(interior)
        def _():
            for k in ks:
                action(k)

        @pl.when(jnp.logical_not(interior))
        def _():
            for k in ks:
                @pl.when(condition(k))
                def _():
                    action(k)

    def spatial_start(group):
        each(range(2), sends, lambda k: spatial(group, k).start())
        if group != "A":
            make_pack(GROUPS[group][0])
        each(range(2, 8), sends, lambda k: spatial(group, k).start())

    def spatial_wait_recv(group):
        each(range(8), receives, lambda k: spatial(group, k).wait_recv())

    def spatial_wait_send(group):
        each(range(8), sends, lambda k: spatial(group, k).wait_send())

    def onward(n):
        src, dst = ((8, 4), (6, 2), (4, 0))[n]
        return pltpu.make_async_remote_copy(
            src_ref=rc.at[pl.ds(src, 2), 2:6], dst_ref=rc.at[pl.ds(dst, 2), 2:6],
            send_sem=ysend.at[n], recv_sem=yrecv.at[n],
            device_id=device(1, 0, 0), device_id_type=MESH,
        )

    row8 = lax.broadcasted_iota(jnp.int32, (8, 1), 0)

    def make_pack(g):
        halves = [[jnp.zeros((8, LAT), F32)] * 2 for _ in range(2)]
        for q in range(R):
            for t2 in range(2):
                half, at = divmod(q * 4 + t2 * 2, 8)
                x = rc[2 * g + t2, 2 + q].astype(F32)
                here = jnp.logical_and(row8 >= at, row8 < at + 2)
                for side, y in ((0, x[0:8]), (1, x[8:16])):
                    by = (at - 6 * side) % 8
                    if by:
                        y = pltpu.roll(y, by, 0)
                    halves[side][half] = jnp.where(here, y, halves[side][half])
        for side in range(2):
            pack[side, g] = jnp.concatenate(halves[side], axis=0).astype(BF16)

    barrier = pltpu.get_barrier_semaphore()
    partners = [(-1, 0, 0)] + [(0, dr, dc) for dr, dc in DIRS] + [(1, 0, 0)]
    for d in partners:
        pl.semaphore_signal(barrier, inc=1, device_id=device(*d), device_id_type=MESH)

    tile = pltpu.make_async_copy(latent, rc.at[6:10, 2:6], local.at[0])
    tile.start()
    sel_copy = pltpu.make_async_copy(sel_hbm, sel_ref, local.at[9])
    sel_copy.start()
    second_copy = pltpu.make_async_copy(w2_hbm, w2, local.at[1])
    second_copy.start()
    first_copy = pltpu.make_async_copy(w1_hbm, w1, local.at[2])
    first_copy.start()
    third_copies = []
    for n, (e, p, fi, fo) in enumerate(
        [(0, 0, 0, 0), (1, 0, 1, 0), (0, 0, 1, 1), (2, 1, 0, 0), (1, 1, 0, 1), (2, 1, 1, 1)]
    ):
        copy = pltpu.make_async_copy(
            w3_hbm.at[:, :, e],
            w3e.at[:, p, :, fi * MID : (fi + 1) * MID, fo * MID : (fo + 1) * MID],
            local.at[3 + n],
        )
        copy.start()
        third_copies.append(copy)

    tile.wait()
    make_pack(4)
    make_pack(3)
    pl.semaphore_wait(barrier, len(partners))

    @pl.when(s < sections - 1)
    def _():
        onward(0).start()

    spatial_start("A")

    @pl.when(s < sections - 1)
    def _():
        onward(1).start()

    @pl.when(r == 0)
    def _():
        rc[:, 0:2] = jnp.zeros((10, 2, C, LAT), BF16)
        halo[:, 0] = jnp.zeros((2, 5, 16, LAT), BF16)

    @pl.when(r == rows - 1)
    def _():
        rc[:, 6:8] = jnp.zeros((10, 2, C, LAT), BF16)
        halo[:, 2] = jnp.zeros((2, 5, 16, LAT), BF16)

    @pl.when(c == 0)
    def _():
        halo[0] = jnp.zeros((3, 5, 16, LAT), BF16)

    @pl.when(c == cols - 1)
    def _():
        halo[1] = jnp.zeros((3, 5, 16, LAT), BF16)

    @pl.when(s == 0)
    def _():
        rc[2:6] = jnp.zeros((4, 8, C, LAT), BF16)
        halo[:, :, 1:3] = jnp.zeros((2, 3, 2, 16, LAT), BF16)

    @pl.when(s <= 1)
    def _():
        rc[0:2] = jnp.zeros((2, 8, C, LAT), BF16)
        halo[:, :, 0:1] = jnp.zeros((2, 3, 1, 16, LAT), BF16)

    w3e[:, 0, :, 0:MID, MID:] = jnp.zeros((3, 3, MID, MID), BF16)
    w3e[:, 1, :, MID:, 0:MID] = jnp.zeros((3, 3, MID, MID), BF16)

    second_copy.wait()
    pick = {(0, 0): (0, 1), (0, 1): (2,), (1, 0): (0,), (1, 1): (1, 2)}

    @pl.loop(0, 3)
    def _(a):
        for fr in range(2):
            for q in range(2):
                column = []
                for e in range(3):
                    x = [w2[a, b, e].astype(F32) for b in pick[fr, q]]
                    column.append(functools.reduce(jnp.add, x))
                for fc in range(2):
                    for p in range(2):
                        x = functools.reduce(jnp.add, [column[e] for e in pick[fc, p]])
                        lane = (fr * 2 + fc) * MID
                        row = (q * 2 + p) * LAT
                        w2e[a, row : row + LAT, lane : lane + MID] = x.astype(BF16)

    def prepare(g):
        left = [halo[0, slot, g].astype(F32) for slot in range(3)]
        for t2 in range(2):
            t = 2 * g + t2
            rhs = jnp.concatenate([rc[t].reshape(8 * C, LAT), halo[1, :, g].reshape(48, LAT)], axis=0)
            moved = jnp.dot(sel_ref[t2], rhs, preferred_element_type=F32).astype(BF16)
            for tap in range(9):
                e9[t, :, tap * LAT : (tap + 1) * LAT] = moved[tap * 16 : tap * 16 + 16]
            for row in range(8):
                slot, k = (0, row + 2) if row < 2 else (1, row - 2) if row < 6 else (2, row - 6)
                k = k * 4 + t2 * 2
                x = pltpu.roll(rc[t, row].astype(F32), 1, 0)
                x = jnp.where(row16 == 0, left[slot][k + 1 : k + 2], x)
                m1[t, row] = x.astype(BF16)
                x = jnp.where(row16 == 0, left[slot][k : k + 1], pltpu.roll(x, 1, 0))
                m0[t, row] = x.astype(BF16)

    row16 = lax.broadcasted_iota(jnp.int32, (16, 1), 0)
    top, bottom = r == 0, r == rows - 1
    leftmost, rightmost = c == 0, c == cols - 1

    def shifted_up(x, last):
        return jnp.where(row16 == 15, last, pltpu.roll(x, 15, 0))

    def conv1(f):
        shifts = (m0, m1, rc)
        blocks = []
        for a in range(3):
            for tap, (dr, dc) in enumerate(TAPS):
                x = shifts[dc]
                blocks.append(
                    jnp.concatenate(
                        [x[f + a, dr : dr + 6].reshape(96, LAT), x[f + 1 + a, dr : dr + 6].reshape(96, LAT),
                         e9[f + a, :, tap * LAT : (tap + 1) * LAT], e9[f + 1 + a, :, tap * LAT : (tap + 1) * LAT]],
                        axis=0,
                    )
                )
        lhs = jnp.concatenate(blocks, axis=1)
        total = jnp.dot(lhs, w1[...].reshape(27 * LAT, LAT), preferred_element_type=F32)
        total = jnp.maximum(total, 0.0)
        for i in range(2):
            main = total[i * 96 : i * 96 + 96].reshape(6, 16, LAT)
            edge = total[192 + i * 16 : 208 + i * 16]
            row8 = row16 % 8
            bad = jnp.logical_or(
                jnp.logical_or(jnp.logical_and(row8 == 0, top), jnp.logical_and(row8 == 5, bottom)),
                jnp.logical_and(row16 >= 8, rightmost),
            )
            edge = jnp.where(jnp.logical_or(bad, row8 >= 6), 0.0, edge)
            for q in range(6):
                bad = jnp.logical_and(row16 == 0, leftmost)
                if q == 0:
                    bad = jnp.logical_or(bad, top)
                if q == 5:
                    bad = jnp.logical_or(bad, bottom)
                x = jnp.where(bad, 0.0, main[q])
                f0[f + i, q] = x.astype(BF16)
                f1[f + i, q] = shifted_up(x, edge[q : q + 1]).astype(BF16)
            nothing = jnp.zeros((8, LAT), F32)
            for p in range(2):
                x = edge[p * 8 : p * 8 + 8]
                for q, y in ((0, x), (1, pltpu.roll(x, 7, 0))):
                    lane = (q * 2 + p) * LAT
                    e2[f + i, :, lane : lane + LAT] = jnp.concatenate([y, nothing], axis=0).astype(BF16)

    def conv2(f):
        shifts = (f0, f1)
        blocks = []
        for a in range(3):
            for q in range(2):
                for p in range(2):
                    x = shifts[p]
                    lane = (q * 2 + p) * LAT
                    blocks.append(
                        jnp.concatenate(
                            [x[f + a, q : q + 5].reshape(80, LAT), x[f + 1 + a, q : q + 5].reshape(80, LAT),
                             e2[f + a, :, lane : lane + LAT], e2[f + 1 + a, :, lane : lane + LAT]],
                            axis=0,
                        )
                    )
        lhs = jnp.concatenate(blocks, axis=1)
        total = jnp.dot(lhs, w2e[...].reshape(12 * LAT, 4 * MID), preferred_element_type=F32)
        total = jnp.maximum(total, 0.0)
        for i in range(2):
            for lane in range(4):
                fr, fc = lane // 2, lane % 2
                cut = slice(lane * MID, (lane + 1) * MID)
                edge = total[160 + i * 16 : 176 + i * 16, cut]
                bad = jnp.logical_and(row16 == (0 if fr == 0 else 4), top if fr == 0 else bottom)
                if fc == 1:
                    bad = jnp.logical_or(bad, rightmost)
                edge = jnp.where(bad, 0.0, edge)
                for q in range(5):
                    x = total[i * 80 + q * 16 : i * 80 + q * 16 + 16, cut]
                    if fc == 0:
                        x = jnp.where(jnp.logical_and(row16 == 0, leftmost), 0.0, x)
                    if fr == 0 and q == 0:
                        x = jnp.where(top, 0.0, x)
                    if fr == 1 and q == 4:
                        x = jnp.where(bottom, 0.0, x)
                    s0[f + i, q, :, cut] = x.astype(BF16)
                    s1[f + i, q, :, cut] = shifted_up(x, edge[q : q + 1]).astype(BF16)

    def conv3(f):
        shifts = (s0, s1)
        blocks = []
        for a in range(3):
            for p in range(2):
                for b in range(3):
                    parts = []
                    for parity in range(2):
                        q, fr = divmod(b + parity, 2)
                        for i in range(2):
                            x = shifts[p][f + i + a, q : q + 4, :, fr * 256 : fr * 256 + 256]
                            parts.append(x.reshape(64, 256))
                    blocks.append(jnp.concatenate(parts, axis=0))
        lhs = jnp.concatenate(blocks, axis=1)
        total = jnp.dot(lhs, w3e[...].reshape(18 * 256, 256), preferred_element_type=F32)
        for parity in range(2):
            for i in range(2):
                for q in range(4):
                    at = parity * 128 + i * 64 + q * 16
                    for fc in range(2):
                        woven[fc::2] = total[at : at + 16, fc * MID : (fc + 1) * MID]
                    out_ref[f + i, 2 * q + parity] = woven[...].astype(BF16)

    @pl.when(s > 0)
    def _():
        onward(0).wait_recv()

        @pl.when(s < sections - 1)
        def _():
            onward(2).start()

        spatial_start("B1")

    sel_copy.wait()
    spatial_wait_recv("A")

    @pl.loop(0, 4)
    def _(i):
        f = 6 - 2 * i

        @pl.when(jnp.logical_and(i == 1, s > 0))
        def _():
            onward(1).wait_recv()
            spatial_start("B0")
            spatial_wait_recv("B1")

        @pl.when(jnp.logical_and(i == 2, s > 0))
        def _():
            spatial_wait_recv("B0")

        @pl.when(jnp.logical_and(i == 3, s > 1))
        def _():
            spatial_wait_recv("C")

        @pl.loop(jnp.where(i == 0, 0, 1), 2)
        def _(k):
            prepare(4 - i - k)

        @pl.when(i == 0)
        def _():
            first_copy.wait()

        conv1(f)

        @pl.when(jnp.logical_and(i == 1, s > 1))
        def _():
            onward(2).wait_recv()
            spatial_start("C")

        @pl.when(i >= 1)
        def _():
            conv2(f)

        @pl.when(i == 2)
        def _():
            for copy in third_copies:
                copy.wait()

        @pl.when(i >= 2)
        def _():
            conv3(f)


    spatial_wait_send("A")

    @pl.when(s < sections - 1)
    def _():
        onward(0).wait_send()
        onward(1).wait_send()

    @pl.when(s > 0)
    def _():
        spatial_wait_send("B1")
        spatial_wait_send("B0")

        @pl.when(s < sections - 1)
        def _():
            onward(2).wait_send()

    @pl.when(s > 1)
    def _():
        spatial_wait_send("C")


def solution(mesh):
    sizes = tuple(mesh.shape[a] for a in ("section", "row", "col"))
    sel = selections()

    def per_device(latent, w_first, w_second, w_third):
        hbm = pl.BlockSpec(memory_space=pltpu.HBM)
        vmem = pl.BlockSpec(memory_space=pltpu.VMEM)
        out = pl.pallas_call(
            functools.partial(kernel, sizes),
            out_shape=pltpu.VMEM((T, 2 * R, 2 * C, MID), BF16),
            in_specs=[hbm] * 5,
            out_specs=vmem,
            scratch_shapes=[
                pltpu.VMEM((10, 8, C, LAT), BF16),
                pltpu.VMEM((2, 3, 5, 16, LAT), BF16),
                pltpu.VMEM((2, 5, 16, LAT), BF16),
                pltpu.VMEM((10, 8, C, LAT), BF16),
                pltpu.VMEM((10, 8, C, LAT), BF16),
                pltpu.VMEM((10, 16, 9 * LAT), BF16),
                pltpu.VMEM((8, 6, 16, LAT), BF16),
                pltpu.VMEM((8, 6, 16, LAT), BF16),
                pltpu.VMEM((8, 16, 4 * LAT), BF16),
                pltpu.VMEM((6, 5, 16, 4 * MID), BF16),
                pltpu.VMEM((6, 5, 16, 4 * MID), BF16),
                pltpu.VMEM((3, 3, 3, LAT, LAT), BF16),
                pltpu.VMEM((3, 3, 3, LAT, MID), BF16),
                pltpu.VMEM((3, 4 * LAT, 4 * MID), BF16),
                pltpu.VMEM((3, 2, 3, 2 * MID, 2 * MID), BF16),
                pltpu.VMEM((2, 144, 176), BF16),
                pltpu.VMEM((2 * C, MID), F32),
                pltpu.SemaphoreType.DMA((4, 8)),
                pltpu.SemaphoreType.DMA((4, 8)),
                pltpu.SemaphoreType.DMA((3,)),
                pltpu.SemaphoreType.DMA((3,)),
                pltpu.SemaphoreType.DMA((10,)),
            ],
            compiler_params=pltpu.CompilerParams(
                collective_id=0, has_side_effects=True, vmem_limit_bytes=56 * 1024 * 1024
            ),
            cost_estimate=pl.CostEstimate(flops=7 * 10**9, bytes_accessed=8 * 10**6, transcendentals=0),
            name="decoder_block",
        )(latent, w_first, w_second, w_third, jnp.asarray(sel))
        return out

    spec = P("section", "row", "col", None)
    return jax.shard_map(
        per_device, mesh=mesh, in_specs=(spec, P(), P(), P()), out_specs=spec, check_vma=False
    )
```
